256 devices in a mesh: row: 8 (over z), col: 32 (over y, x, core).
Axes of the slice: x: 4, y: 4, z: 8, core: 2. Of those that a mesh axis runs over, the one named last changes fastest.
Arguments:
- tokens: bfloat16 [1536, 4096], P('row', 'col'), may hold values from -6 to 6
- w_in: bfloat16 [4096, 12288], P('row', 'col'), may hold values from -0.09375 to 0.09375
- bias_in: float32 [12288], P('col'), may hold values from -3 to 3
- w_out: bfloat16 [12288, 4096], P('row', 'col'), may hold values from -0.0546875 to 0.0546875
- grad_out: bfloat16 [1536, 4096], P('row', 'col'), may hold values from -1.5 to 1.5
Outputs:
- block_out: bfloat16 [1536, 4096], P('row', 'col')
- grad_tokens: bfloat16 [1536, 4096], P('row', 'col')
- grad_w_in: float32 [4096, 12288], P('row', 'col')
- grad_bias: float32 [12288], P('col')
- grad_w_out: float32 [12288, 4096], P('row', 'col')
The draws below stay inside these ranges and needn't reach their ends.
All inputs are finite; a program needn't handle non-finite values.
Results may differ from the reference program's by a relative error of at most 0.029.
Values may be sent and summed in bfloat16 or wider, within the bound.
A program may use at most 64 MiB of HBM per device.

```python
import jax
import jax.numpy as jnp
from jax import lax

D = 4096
FF = 12288
TOKENS = 1536
N_COL = 32


def levels(stream_key, extent, shards, low, largest):
    level, own = 1.0, jax.random.fold_in(stream_key, 6)
    for position, shards_of in shards:
        steps = jnp.exp(jax.random.uniform(jax.random.fold_in(own, position), (shards_of,), jnp.float32, low / len(shards), largest / len(shards)))
        level = level * jnp.repeat(steps, extent[position] // shards_of).reshape([-1 if axis == position else 1 for axis in range(len(extent))])
    return level


def bell_draw(own_key, dims, spread, limit, cuts=(), held_as=jnp.bfloat16):
    drawn = jax.random.normal(own_key, dims, jnp.float32) * spread
    if len(cuts) > 0:
        drawn = levels(own_key, dims, cuts, -0.22, 0.18) * drawn
    return jnp.clip(drawn, min=-limit, max=limit).astype(held_as)


def setup_inputs(seed: int = 0) -> dict:
    seeds = jax.random.split(jax.random.key(seed), 6)
    tokens = bell_draw(seeds[0], (TOKENS, D), 1.0, 6.0, ((0, 8), (1, 32)))
    w_in = bell_draw(seeds[1], (D, FF), D ** -0.5, 0.09375, ((0, 8), (1, 32)))
    bias_in = bell_draw(seeds[2], (FF,), 0.5, 3.0, ((0, 32),), jnp.float32)
    w_out = bell_draw(seeds[3], (FF, D), FF ** -0.5, 0.0546875, ((0, 8), (1, 32)))
    grad_out = bell_draw(seeds[4], (TOKENS, D), 0.25, 1.5, ((0, 8), (1, 32)))
    return dict(tokens=tokens, w_in=w_in, bias_in=bias_in, w_out=w_out, grad_out=grad_out)


def reference(tokens, w_in, bias_in, w_out, grad_out):
    preact = jnp.dot(tokens, w_in, preferred_element_type=jnp.float32) + bias_in
    hidden = jax.nn.gelu(preact).astype(jnp.bfloat16)
    block_out = jnp.dot(hidden, w_out, preferred_element_type=jnp.float32).astype(jnp.bfloat16)
    feature_cols = D // N_COL
    hidden_cols = FF // N_COL
    blocks = jnp.arange(N_COL, dtype=jnp.int32)

    def add_hidden(carry, block_index):
        lower = block_index * feature_cols
        grads_block = lax.dynamic_slice_in_dim(grad_out, lower, feature_cols, 1)
        weight_block = lax.dynamic_slice_in_dim(w_out, lower, feature_cols, 1)
        term = lax.dot_general(grads_block, weight_block, (((1,), (1,)), ((), ())), preferred_element_type=jnp.float32)
        rounded = lax.optimization_barrier(term.astype(jnp.bfloat16))
        return (carry + rounded.astype(jnp.float32), None)
    grad_hidden = lax.scan(add_hidden, jnp.zeros((TOKENS, FF), jnp.float32), blocks)[0]
    grad_pre = jax.vjp(jax.nn.gelu, preact)[1](grad_hidden)[0].astype(jnp.bfloat16)

    def add_input(carry, block_index):
        lower = block_index * hidden_cols
        grads_block = lax.dynamic_slice_in_dim(grad_pre, lower, hidden_cols, 1)
        weight_block = lax.dynamic_slice_in_dim(w_in, lower, hidden_cols, 1)
        term = lax.dot_general(grads_block, weight_block, (((1,), (1,)), ((), ())), preferred_element_type=jnp.float32)
        rounded = lax.optimization_barrier(term.astype(jnp.bfloat16))
        return (carry + rounded.astype(jnp.float32), None)
    input_total = lax.scan(add_input, jnp.zeros((TOKENS, D), jnp.float32), blocks)[0]
    grad_tokens = input_total.astype(jnp.bfloat16)
    grad_w_in = lax.dot_general(tokens, grad_pre, (((0,), (0,)), ((), ())), preferred_element_type=jnp.float32)
    grad_bias = lax.optimization_barrier(jnp.sum(grad_pre.astype(jnp.float32), axis=0))
    grad_w_out = lax.dot_general(hidden, grad_out, (((0,), (0,)), ((), ())), preferred_element_type=jnp.float32)
    return (block_out, grad_tokens, grad_w_in, grad_bias, grad_w_out)
```

```python
import functools

import jax
import jax.numpy as jnp
from jax import lax
from jax.experimental import pallas as pl
from jax.experimental.pallas import tpu as pltpu
from jax.sharding import PartitionSpec as P

MESH = pl.DeviceIdType.MESH
BF, F32 = jnp.bfloat16, jnp.float32
S2PI = 0.7978845608028654
CUBIC = 0.044715


def dot(a, b):
    return lax.dot_general(a, b, (((1,), (0,)), ((), ())), preferred_element_type=F32)


def dot_t(a, b):
    return lax.dot_general(a, b, (((1,), (1,)), ((), ())), preferred_element_type=F32)


def t_dot(a, b):
    return lax.dot_general(a, b, (((0,), (0,)), ((), ())), preferred_element_type=F32)


def col(y, x, k):
    return y * 8 + x * 2 + k


def lanes(i, n):
    return pl.ds(pl.multiple_of(i * n, n), n)


def kernel(
    tok, w1, bias, w2, go,
    out_y, out_x, out_w1, out_b, out_w2,
    xa, xg, w1g, w2g, gs, gg, b8, bg,
    ps, pr, dhs, dhr, ho, dpo, hg, dpg,
    ys, ya, yb, yr, d2s, d2r, dxs, dxr, dxb, ot, d1s, d1r, bs, dbr,
    send, x1_r, x2_r, w1_r, w2_r, b_r, g1_r, g2_r, g3_r, p_r, dh_r, h_r, dp_r,
    y1_r, y2_r, d2_r, dx1_r, dx2_r, d1_r, db_r,
):
    z, c = lax.axis_index("row"), lax.axis_index("col")
    k, x, y = c % 2, (c // 2) % 4, c // 8
    sent = []

    def put(src, dst, rsem, dev):
        i = len(sent)
        copy = pltpu.make_async_remote_copy(
            src_ref=src, dst_ref=dst, send_sem=send.at[i], recv_sem=rsem,
            device_id=dev, device_id_type=MESH,
        )
        copy.start()
        sent.append((copy, None))

    def put_if(cond, src, dst, rsem, dev):
        i = len(sent)
        copy = pltpu.make_async_remote_copy(
            src_ref=src, dst_ref=dst, send_sem=send.at[i], recv_sem=rsem,
            device_id=dev, device_id_type=MESH,
        )
        pl.when(cond)(copy.start)
        sent.append((copy, cond))

    def put_any(src, dst, rsem, dev, here):
        put_if(jnp.logical_not(here), src, dst, rsem, dev)
        pl.when(here)(pltpu.make_async_copy(src, dst, rsem).start)

    def keep(src, dst, rsem):
        pltpu.make_async_copy(src, dst, rsem).start()

    def got(dst, rsem):
        pltpu.make_async_copy(dst, dst, rsem).wait()

    barrier = pltpu.get_barrier_semaphore()
    near = [((z + i) % 8, c) for i in range(1, 8)]
    near += [(z, col((y + i) % 4, x, (k + d) % 2)) for i in range(4) for d in range(2) if i or d]
    near += [(z, col(y, (x + i) % 4, (k + d) % 2)) for i in range(1, 4) for d in range(2)]
    far = [(2 * y + x // 2, col(z // 2, j, x % 2)) for j in range(4)]
    back = [(2 * y + h, col(z // 2, 2 * (z % 2) + k, d)) for h in range(2) for d in range(2)]
    for dev in near + far + back:
        pl.semaphore_signal(barrier, inc=1, device_id=dev, device_id_type=MESH)
    pl.semaphore_wait(barrier, len(near + far + back))

    for j in range(4):
        here = jnp.logical_and(far[j][0] == z, far[j][1] == c)
        put_any(
            tok.at[pl.ds(j * 48, 48)], xa.at[z % 2, :, lanes(k, 128)], x1_r.at[z % 2, k], far[j], here
        )
    at_row = y == z // 2
    put_any(go, gs.at[:, lanes(y, 128)], g1_r.at[y], (z, col(z // 2, x, k)), at_row)
    b8[...] = jnp.broadcast_to(bias[...], b8.shape)
    keep(w1, w1g.at[y], w1_r.at[y])
    keep(b8, bg.at[y], b_r.at[y])
    half = [w2.at[lanes((k + d) % 2, 768)] for d in range(2)]
    keep(half[0], w2g.at[k, :, lanes(y, 128)], w2_r.at[y, k])
    put(half[1], w2g.at[k, :, lanes(y, 128)], w2_r.at[y, k], (z, col(y, x, 1 - k)))
    for i in (1, 3, 2):
        put(w1, w1g.at[y], w1_r.at[y], (z, col((y + i) % 4, x, k)))
        put(b8, bg.at[y], b_r.at[y], (z, col((y + i) % 4, x, k)))
    for i in (1, 3, 2):
        for d in range(2):
            put(
                half[d], w2g.at[k, :, lanes(y, 128)], w2_r.at[y, k],
                (z, col((y + i) % 4, x, (k + d) % 2)),
            )

    for h in range(2):
        for d in range(2):
            got(xa.at[h, :, pl.ds(d * 128, 128)], x1_r.at[h, d])
    keep(xa, xg.at[k, :, x], x2_r.at[x, k])
    for i in range(4):
        for d in range(2):
            if i or d:
                put(xa, xg.at[k, :, x], x2_r.at[x, k], (z, col(y, (x + i) % 4, (k + d) % 2)))

    @pl.when(at_row)
    def _():
        for i in range(4):
            got(gs.at[:, pl.ds(i * 128, 128)], g1_r.at[i])
        keep(gs, gg.at[k, z % 2], g2_r.at[z % 2])

    for i in (4, 3, 5, 2, 6, 1, 7):
        put_if(at_row, gs, gg.at[k, z % 2], g2_r.at[z % 2], ((z + i) % 8, c))

    for i in range(4):
        for d in range(2):
            got(xg.at[d, :, i], x2_r.at[i, d])
    for i in range(4):
        got(w1g.at[i], w1_r.at[i])

    def part(i, _):
        x0 = xg[0].reshape(384, 256)
        x1 = xg[1].reshape(384, 256)
        ps[i] = (dot(x0, w1g[i, :256]) + dot(x1, w1g[i, 256:])).astype(BF)
        return 0

    owner = z % 2 == x // 2
    lax.fori_loop(0, 4, part, 0)
    for i in range(4):
        dest = 2 * i + x // 2
        put_any(ps.at[i], pr.at[z], p_r.at[z], (dest, c), dest == z)

    for h in range(2):
        got(gg.at[k, h], g2_r.at[h])
    put(gg.at[k], gg.at[k], g3_r, (z, col(y, x, 1 - k)))
    got(gg.at[1 - k], g3_r)
    for i in range(4):
        for d in range(2):
            got(w2g.at[d, :, pl.ds(i * 128, 128)], w2_r.at[i, d])

    def part_hidden(i, _):
        rows = pl.ds(pl.multiple_of(i * 384, 384), 384)
        g0 = gg[0].reshape(384, 512)
        g1 = gg[1].reshape(384, 512)
        dhs[i] = (dot_t(g0, w2g[0, rows, :]) + dot_t(g1, w2g[1, rows, :])).astype(BF)
        return 0

    lax.fori_loop(0, 2, part_hidden, 0)
    home = 2 * (z % 2) + k
    for i in range(2):
        put_any(
            dhs.at[i], dhr.at[x], dh_r.at[x], (z, col(y, home, i)),
            jnp.logical_and(home == x, k == i),
        )

    @pl.when(owner)
    def _():
        for i in range(4):
            got(bg.at[i], b_r.at[i])
        for i in range(8):
            got(pr.at[i], p_r.at[i])
        for i in range(4):
            got(dhr.at[i], dh_r.at[i])

        def point(i, _):
            rows = pl.ds(pl.multiple_of(i * 16, 16), 16)
            v = jnp.broadcast_to(bg[z // 2, pl.ds(0, 1), :], (16, 384))
            for j in range(8):
                v = v + pr[j, rows, :].astype(F32)
            up = dhr[0, rows, :].astype(F32)
            for j in range(1, 4):
                up = up + dhr[j, rows, :].astype(F32)
            v2 = v * v
            t = jnp.tanh(S2PI * (v + CUBIC * (v2 * v)))
            cdf = 0.5 * (1.0 + t)
            ho[rows, :] = (v * cdf).astype(BF)
            slope = cdf + (0.5 * v) * (1.0 - t * t) * (S2PI * (1.0 + 3.0 * CUBIC * v2))
            dpo[rows, :] = (up * slope).astype(BF)
            return 0

        lax.fori_loop(0, 24, point, 0)
        keep(dpo, dpg.at[z // 2], dp_r.at[z // 2])

    @pl.when(jnp.logical_not(owner))
    def _():
        for i in range(4):
            got(bg.at[i], b_r.at[i])

    for i in range(4):
        put_any_if = jnp.logical_and((x + i) % 4 == x, x % 2 == k)
        dev = (z, col(y, (x + i) % 4, x % 2))
        put_if(jnp.logical_and(owner, jnp.logical_not(put_any_if)), ho, hg.at[k], h_r.at[k], dev)
        pl.when(jnp.logical_and(owner, put_any_if))(
            pltpu.make_async_copy(ho, hg.at[k], h_r.at[k]).start
        )
    for i in (4, 3, 5, 2, 6, 1, 7):
        put_if(owner, dpo, dpg.at[z // 2], dp_r.at[z // 2], ((z + i) % 8, c))

    for i in range(2):
        got(hg.at[i], h_r.at[i])

    def part_out(i, _):
        o = dot(hg[0], w2g[i, :384, :]) + dot(hg[1], w2g[i, 384:, :])
        for j in range(4):
            ys[i, j] = o[:, j * 128:(j + 1) * 128].astype(BF)
        return 0

    lax.fori_loop(0, 2, part_out, 0)
    for i in range(4):
        for d in range(2):
            dy, dk = (y + i) % 4, (k + d) % 2
            if i or d:
                put(ys.at[dk, dy], ya.at[y, k], y1_r.at[y, k], (z, col(dy, x, dk)))
            else:
                keep(ys.at[dk, dy], ya.at[y, k], y1_r.at[y, k])

    def part_w2(i, _):
        g = gg[i].reshape(384, 512)
        for r in range(2):
            o = t_dot(hg[r], g)
            for j in range(4):
                d2s[i, j, pl.ds(r * 384, 384), :] = o[:, j * 128:(j + 1) * 128].astype(BF)
        return 0

    lax.fori_loop(0, 2, part_w2, 0)
    for i in (0, 1, 3, 2):
        for d in range(2):
            dy, dk = (y + i) % 4, (k + d) % 2
            if i or d:
                put(d2s.at[dk, dy], d2r.at[y, k], d2_r.at[y, k], (z, col(dy, x, dk)))
            else:
                keep(d2s.at[dk, dy], d2r.at[y, k], d2_r.at[y, k])

    for i in range(4):
        got(dpg.at[i], dp_r.at[i])
    for i in range(2):
        o = dot_t(dpg[0], w1g[0, pl.ds(i * 256, 256), :])
        for j in range(1, 4):
            o = o + dot_t(dpg[j], w1g[j, pl.ds(i * 256, 256), :])
        dxs[i] = o.astype(BF).reshape(2, 4, 48, 256)
    for i in range(4):
        for d in range(2):
            dx, dk = (x + i) % 4, (k + d) % 2
            if i or d:
                put(dxs.at[dk, :, dx], dxr.at[x, k], dx1_r.at[x, k], (z, col(y, dx, dk)))
            else:
                keep(dxs.at[dk, :, dx], dxr.at[x, k], dx1_r.at[x, k])

    def part_w1(i, _):
        for r in range(2):
            d1s[i, pl.ds(r * 256, 256), :] = t_dot(xg[r].reshape(384, 256), dpg[i]).astype(BF)
        total = jnp.sum(dpg[i].astype(F32), axis=0, keepdims=True)
        bs[i] = jnp.broadcast_to(total, (8, 384))
        return 0

    lax.fori_loop(0, 4, part_w1, 0)
    keep(d1s.at[y], d1r.at[y], d1_r.at[y])
    keep(bs.at[y], dbr.at[y], db_r.at[y])
    for i in (1, 3, 2):
        dy = (y + i) % 4
        put(d1s.at[dy], d1r.at[y], d1_r.at[y], (z, col(dy, x, k)))
        put(bs.at[dy], dbr.at[y], db_r.at[y], (z, col(dy, x, k)))

    for i in range(4):
        for d in range(2):
            got(ya.at[i, d], y1_r.at[i, d])
    for i in range(8):
        rows = pl.ds((i % 2) * 192, 192)
        yb[i] = (ya[i // 2, 0, rows, :].astype(F32) + ya[i // 2, 1, rows, :].astype(F32)).astype(BF)
    for i in range(8):
        j = (z + i) % 8
        if i:
            put(yb.at[j], yr.at[z], y2_r.at[z], (j, c))
        else:
            keep(yb.at[j], yr.at[z], y2_r.at[z])

    for i in range(4):
        for d in range(2):
            got(dxr.at[i, d], dx1_r.at[i, d])
    for h in range(2):
        o = dxr[0, 0, h].astype(F32)
        for j in range(1, 8):
            o = o + dxr[j // 2, j % 2, h].astype(F32)
        for d in range(2):
            dxb[h, d] = o[:, d * 128:(d + 1) * 128].astype(BF)
    for h in range(2):
        for d in range(2):
            dev = back[2 * h + d]
            put_any(
                dxb.at[h, d], ot.at[x], dx2_r.at[x], dev,
                jnp.logical_and(dev[0] == z, dev[1] == c),
            )

    for i in range(4):
        for d in range(2):
            got(d2r.at[i, d], d2_r.at[i, d])

    def sum_w2(i, _):
        for d in range(2):
            rows = pl.ds(pl.multiple_of(i * 64, 64), 64)
            o = d2r[0, d, rows, :].astype(F32)
            for j in range(1, 4):
                o = o + d2r[j, d, rows, :].astype(F32)
            out_w2[pl.ds(pl.multiple_of(d * 768 + i * 64, 64), 64), :] = o
        return 0

    lax.fori_loop(0, 12, sum_w2, 0)
    for i in range(8):
        got(yr.at[i], y2_r.at[i])
    o = yr[0].astype(F32)
    for j in range(1, 8):
        o = o + yr[j].astype(F32)
    out_y[...] = o.astype(BF)
    for i in range(4):
        got(ot.at[i], dx2_r.at[i])
    out_x[...] = ot[...].reshape(192, 128)
    for i in range(4):
        got(d1r.at[i], d1_r.at[i])
        got(dbr.at[i], db_r.at[i])

    def sum_w1(i, _):
        rows = pl.ds(pl.multiple_of(i * 32, 32), 32)
        o = d1r[0, rows, :].astype(F32)
        for j in range(1, 4):
            o = o + d1r[j, rows, :].astype(F32)
        out_w1[rows, :] = o
        return 0

    lax.fori_loop(0, 16, sum_w1, 0)
    o = dbr[0] + dbr[1] + dbr[2] + dbr[3]
    out_b[...] = o[:1]

    for copy, cond in sent:
        if cond is None:
            copy.wait_send()
        else:
            pl.when(cond)(copy.wait_send)


SENDS = 160
DMA = pltpu.SemaphoreType.DMA


def per_device(tokens, w_in, bias_in, w_out, grad_out):
    vm = pltpu.VMEM
    spec = pl.BlockSpec(memory_space=pltpu.VMEM)
    shapes = [
        ((192, 128), BF), ((192, 128), BF), ((512, 384), F32), ((1, 384), F32), ((1536, 128), F32),
    ]
    out = pl.pallas_call(
        kernel,
        out_shape=[jax.ShapeDtypeStruct(s, d) for s, d in shapes],
        in_specs=[spec] * 5,
        out_specs=[spec] * 5,
        scratch_shapes=[
            vm((2, 48, 256), BF),
            vm((2, 2, 4, 48, 256), BF),
            vm((4, 512, 384), BF),
            vm((2, 768, 512), BF),
            vm((192, 512), BF),
            vm((2, 2, 192, 512), BF),
            vm((8, 384), F32),
            vm((4, 8, 384), F32),
            vm((4, 384, 384), BF),
            vm((8, 384, 384), BF),
            vm((2, 384, 384), BF),
            vm((4, 384, 384), BF),
            vm((384, 384), BF),
            vm((384, 384), BF),
            vm((2, 384, 384), BF),
            vm((4, 384, 384), BF),
            vm((2, 4, 384, 128), BF),
            vm((4, 2, 384, 128), BF),
            vm((8, 192, 128), BF),
            vm((8, 192, 128), BF),
            vm((2, 4, 768, 128), BF),
            vm((4, 2, 768, 128), BF),
            vm((2, 2, 4, 48, 256), BF),
            vm((4, 2, 2, 48, 256), BF),
            vm((2, 2, 48, 128), BF),
            vm((4, 48, 128), BF),
            vm((4, 512, 384), BF),
            vm((4, 512, 384), BF),
            vm((4, 8, 384), F32),
            vm((4, 8, 384), F32),
            DMA((SENDS,)),
            DMA((2, 2)), DMA((4, 2)), DMA((4,)), DMA((4, 2)), DMA((4,)),
            DMA((4,)), DMA((2,)), DMA, DMA((8,)), DMA((4,)), DMA((2,)), DMA((4,)),
            DMA((4, 2)), DMA((8,)), DMA((4, 2)), DMA((4, 2)), DMA((4,)), DMA((4,)), DMA((4,)),
        ],
        compiler_params=pltpu.CompilerParams(
            collective_id=0, has_side_effects=True, vmem_limit_bytes=56 * 2**20
        ),
        name="mlp_grad",
    )(tokens, w_in, bias_in.reshape(1, 384), w_out, grad_out)
    block_out, grad_tokens, grad_w_in, grad_bias, grad_w_out = out
    return block_out, grad_tokens, grad_w_in, grad_bias.reshape(384), grad_w_out


def solution(mesh):
    return jax.shard_map(
        per_device,
        mesh=mesh,
        in_specs=(P("row", "col"), P("row", "col"), P("col"), P("row", "col"), P("row", "col")),
        out_specs=(P("row", "col"), P("row", "col"), P("row", "col"), P("col"), P("row", "col")),
        check_vma=False,
    )
```

```python
import functools

import jax
import jax.numpy as jnp
from jax import lax
from jax.experimental import pallas as pl
from jax.experimental.pallas import tpu as pltpu
from jax.sharding import PartitionSpec as P

MESH = pl.DeviceIdType.MESH
BF, F32 = jnp.bfloat16, jnp.float32
S2PI = 0.7978845608028654
CUBIC = 0.044715


def dot(a, b):
    return lax.dot_general(a, b, (((1,), (0,)), ((), ())), preferred_element_type=F32)


def dot_t(a, b):
    return lax.dot_general(a, b, (((1,), (1,)), ((), ())), preferred_element_type=F32)


def t_dot(a, b):
    return lax.dot_general(a, b, (((0,), (0,)), ((), ())), preferred_element_type=F32)


def col(y, x, k):
    return y * 8 + x * 2 + k


def lanes(i, n):
    return pl.ds(pl.multiple_of(i * n, n), n)


def kernel(
    tok, w1, bias, w2, go,
    out_y, out_x, out_w1, out_b, out_w2,
    xa, xg, w1g, w2h, w2g, gs, gg, b8, bg,
    ps, rz, tz, dhs, dhr, ho, hg, dpg,
    ys, yx, ya, yr, d2s, d2x, d2t, d2r, dxs, dxr, dxb, ot, d1s, d1t, d1r, bs, dbr,
    send, x1_r, x2_r, w1_r, w2s_r, w2k_r, w2_r, b_r, g1_r, g2_r, g3_r, p_r, dh_r, h_r, dp_r,
    yx_r, y1_r, y2_r, d2x_r, d2t_r, d2_r, dx1_r, dx2_r, d1t_r, d1_r, db_r,
):
    z, c = lax.axis_index("row"), lax.axis_index("col")
    k, x, y = c % 2, (c // 2) % 4, c // 8
    sent = []

    def put(src, dst, rsem, dev, cond=None, like=None):
        copy = pltpu.make_async_remote_copy(
            src_ref=src, dst_ref=dst, send_sem=send.at[len(sent)], recv_sem=rsem,
            device_id=dev, device_id_type=MESH,
        )
        if cond is None or like is not None:
            copy.start()
        else:
            pl.when(cond)(copy.start)
        sent.append((like or (lambda: src), cond))

    def put_any(src, dst, rsem, dev, here):
        put(src, dst, rsem, dev, jnp.logical_not(here))
        pl.when(here)(pltpu.make_async_copy(src, dst, rsem).start)

    def keep(src, dst, rsem):
        pltpu.make_async_copy(src, dst, rsem).start()

    def got(dst, rsem):
        pltpu.make_async_copy(dst, dst, rsem).wait()

    barrier = pltpu.get_barrier_semaphore()
    near = [((z + i) % 8, c) for i in range(1, 8)]
    near += [(z, col((y + i) % 4, x, (k + d) % 2)) for i in range(4) for d in range(2) if i or d]
    near += [(z, col(y, (x + i) % 4, (k + d) % 2)) for i in range(1, 4) for d in range(2)]
    far = [(2 * y + x // 2, col(z // 2, j, x % 2)) for j in range(4)]
    back = [(2 * y + h, col(z // 2, 2 * (z % 2) + k, d)) for h in range(2) for d in range(2)]
    for dev in near + far + back:
        pl.semaphore_signal(barrier, inc=1, device_id=dev, device_id_type=MESH)
    pl.semaphore_wait(barrier, len(near + far + back))

    for j in range(4):
        here = jnp.logical_and(far[j][0] == z, far[j][1] == c)
        put_any(
            tok.at[pl.ds(j * 48, 48)], xa.at[z % 2, :, lanes(k, 128)], x1_r.at[z % 2, k], far[j], here
        )
    keep(go, gs.at[z], g1_r.at[z])
    for i in (4, 3, 5, 2, 6, 1, 7):
        put(go, gs.at[z], g1_r.at[z], ((z + i) % 8, c))
    up, down = (y + 1) % 4, (y + 3) % 4
    b8[...] = jnp.broadcast_to(bias[...], b8.shape)
    for i in range(2):
        rows = pl.ds(i * 256, 256)
        keep(w1.at[rows], w1g.at[y, rows], w1_r.at[y, i])
    for i in range(2):
        for n, dy in enumerate((up, down)):
            rows = pl.ds((i ^ n) * 256, 256)
            put(w1.at[rows], w1g.at[y, rows], w1_r.at[y, i ^ n], (z, col(dy, x, k)))
    mine = pl.ds(pl.multiple_of(k * 768, 768), 768)
    theirs = pl.ds(pl.multiple_of((1 - k) * 768, 768), 768)
    put(w2.at[theirs], w2h, w2s_r, (z, col(y, x, 1 - k)))
    keep(w2.at[mine], w2g.at[k, :, lanes(y, 128)], w2k_r)
    keep(b8, bg.at[y], b_r.at[y])
    for i in (1, 2, 3):
        put(b8, bg.at[y], b_r.at[y], (z, col((y + i) % 4, x, k)))
    for h in range(2):
        for d in range(2):
            got(xa.at[h, :, pl.ds(d * 128, 128)], x1_r.at[h, d])
    keep(xa, xg.at[k, :, x], x2_r.at[x, k])
    for i in range(4):
        for d in range(2):
            if i or d:
                put(xa, xg.at[k, :, x], x2_r.at[x, k], (z, col(y, (x + i) % 4, (k + d) % 2)))

    for i, (dy, fy) in enumerate(((up, down), (down, up))):
        rows = pl.ds(i * 256, 256)
        got(w1g.at[fy, rows], w1_r.at[fy, i])
        put(w1g.at[fy, rows], w1g.at[fy, rows], w1_r.at[fy, i], (z, col(dy, x, k)))
    got(w2h, w2s_r)
    keep(w2h, w2g.at[1 - k, :, lanes(y, 128)], w2s_r)
    for i in range(2):
        for dy in (up, down):
            rows = pl.ds(pl.multiple_of(k * 768 + i * 384, 384), 384)
            put(
                w2.at[rows], w2g.at[k, pl.ds(i * 384, 384), lanes(y, 128)], w2_r.at[y, k, i],
                (z, col(dy, x, k)),
            )
            rows = pl.ds(i * 384, 384)
            put(
                w2h.at[rows], w2g.at[1 - k, rows, lanes(y, 128)], w2_r.at[y, 1 - k, i],
                (z, col(dy, x, k)),
            )

    def pass_w2(i):
        for d, (dy, fy) in enumerate(((up, down), (down, up))):
            block = w2g.at[d, pl.ds(i * 384, 384), lanes(fy, 128)]
            got(block, w2_r.at[fy, d, i])
            put(block, block, w2_r.at[fy, d, i], (z, col(dy, x, k)))

    for i in range(8):
        got(gs.at[i], g1_r.at[i])
    for i in (2, 1, 3, 0):
        dy = (y + i) % 4
        src, dst = gs.at[pl.ds(2 * dy, 2)], gg.at[k, :, :, lanes(y, 128)]
        if i:
            put(src, dst, g2_r.at[y], (z, col(dy, x, k)))
        else:
            keep(src, dst, g2_r.at[y])

    for i in range(4):
        for d in range(2):
            got(xg.at[d, :, i], x2_r.at[i, d])
    got(w1g.at[y, pl.ds(0, 256)], w1_r.at[y, 0])
    got(w1g.at[y, pl.ds(256, 256)], w1_r.at[y, 1])
    got(w1g.at[down, pl.ds(256, 256)], w1_r.at[down, 1])
    got(w1g.at[up, pl.ds(0, 256)], w1_r.at[up, 0])
    for i in range(2):
        got(w1g.at[(y + 2) % 4, pl.ds(i * 256, 256)], w1_r.at[(y + 2) % 4, i])

    owner = z % 2 == x // 2
    other = jnp.logical_not(owner)
    odd = (z + x // 2) % 2
    ways = ((1, 0), (-1, 1))
    ahead = [((z + 1) % 8, c), ((z + 7) % 8, c)]

    def block_at(step):
        return ((z + step + 16) % 8) // 2

    first = [block_at(s * (4 - odd)) for s, _ in ways]
    second = [block_at(s * (2 - odd)) for s, _ in ways]

    def piece(j):
        return pl.ds(j * 96, 96)

    def halves(q):
        return (2, 3, 0, 1) if q else (0, 1, 2, 3)

    def part(i, _):
        x0 = xg[0].reshape(384, 256)
        x1 = xg[1].reshape(384, 256)
        ps[i] = (dot(x0, w1g[i, :256]) + dot(x1, w1g[i, 256:])).astype(BF)
        return 0

    lax.fori_loop(0, 4, part, 0)
    for n in range(2):
        for _, q in ways:
            for cond, j in ((owner, halves(q)[n]), (other, halves(q)[2 + n])):
                put(
                    ps.at[first[q], piece(j)], rz.at[q, 0, piece(j)], p_r.at[q, 0, j],
                    ahead[q], cond,
                )
    home = 2 * (z % 2) + k

    def part_hidden(i):
        for d in range(2):
            for j in (down if d else up, (y + 2) % 4):
                got(w2g.at[d, pl.ds(i * 384, 384), lanes(j, 128)], w2_r.at[j, d, i])
        rows = pl.ds(i * 384, 384)
        g0 = gg[0].reshape(384, 512)
        g1 = gg[1].reshape(384, 512)
        dhs[i] = (dot_t(g0, w2g[0, rows, :]) + dot_t(g1, w2g[1, rows, :])).astype(BF)
        put_any(
            dhs.at[i], dhr.at[x], dh_r.at[x], (z, col(y, home, i)),
            jnp.logical_and(home == x, k == i),
        )

    def relay(cond, mine, kind, to, n, q):
        j = (halves(q) if kind == to == 0 else halves(1 - q))[n]
        got(rz.at[q, kind, piece(j)], p_r.at[q, kind, j])
        tz[q, to, piece(j), :] = ps[mine, piece(j), :] + rz[q, kind, piece(j), :]
        put(
            tz.at[q, to, piece(j)], rz.at[q, to, piece(j)], p_r.at[q, to, j], ahead[q], cond,
            lambda: tz.at[q, to, piece(j)],
        )

    for i in range(4):
        got(gg.at[k, :, :, pl.ds(i * 128, 128)], g2_r.at[i])
    put(gg.at[k], gg.at[k], g3_r, (z, col(y, x, 1 - k)))

    @pl.when(other)
    def _():
        for n in range(2):
            for _, q in ways:
                relay(other, first[q], 0, 0, n, q)

    got(w2g.at[k, :, lanes(y, 128)], w2k_r)
    got(w2g.at[1 - k, :, lanes(y, 128)], w2s_r)
    pass_w2(0)

    @pl.when(owner)
    def _():
        for n in range(4):
            for _, q in ways:
                relay(owner, second[q], 0, 1, n, q)

    pass_w2(1)

    got(gg.at[1 - k], g3_r)
    part_hidden(0)
    part_hidden(1)

    @pl.when(other)
    def _():
        for n in range(4):
            for _, q in ways:
                relay(other, second[q], 1, 1, n, q)

    @pl.when(owner)
    def _():
        for i in range(4):
            got(bg.at[i], b_r.at[i])
        for j in range(4):
            for _, q in ways:
                got(rz.at[q, 1, piece(j)], p_r.at[q, 1, j])
        for i in range(4):
            got(dhr.at[i], dh_r.at[i])

        def point(i, _):
            rows = pl.ds(pl.multiple_of(i * 16, 16), 16)
            v = jnp.broadcast_to(bg[z // 2, pl.ds(0, 1), :], (16, 384))
            v = v + ps[z // 2, rows, :].astype(F32)
            v = v + (rz[0, 1, rows, :].astype(F32) + rz[1, 1, rows, :].astype(F32))
            grad = dhr[0, rows, :].astype(F32)
            for j in range(1, 4):
                grad = grad + dhr[j, rows, :].astype(F32)
            v2 = v * v
            t = jnp.tanh(S2PI * (v + CUBIC * (v2 * v)))
            cdf = 0.5 * (1.0 + t)
            ho[rows, :] = (v * cdf).astype(BF)
            slope = cdf + (0.5 * v) * (1.0 - t * t) * (S2PI * (1.0 + 3.0 * CUBIC * v2))
            dpg[z // 2, rows, :] = (grad * slope).astype(BF)
            return 0

        lax.fori_loop(0, 24, point, 0)
        for n in range(4):
            for _, q in ways:
                block = dpg.at[z // 2, piece(halves(q)[n])]
                put(block, block, dp_r.at[z // 2, halves(q)[n]], ahead[q], owner, lambda: dpg.at[0, piece(0)])

    @pl.when(jnp.logical_not(owner))
    def _():
        for i in range(4):
            got(bg.at[i], b_r.at[i])

    for i in range(4):
        here = jnp.logical_and((x + i) % 4 == x, x % 2 == k)
        put(
            ho, hg.at[k], h_r.at[k], (z, col(y, (x + i) % 4, x % 2)),
            jnp.logical_and(owner, jnp.logical_not(here)),
        )
        pl.when(jnp.logical_and(owner, here))(
            pltpu.make_async_copy(ho, hg.at[k], h_r.at[k]).start
        )

    def pass_on(cond, back_by, all_rows):
        for n in range(4):
            for s, q in ways:
                j = halves(q)[n]
                block = dpg.at[block_at(-s * back_by), piece(j)]
                sem = dp_r.at[block_at(-s * back_by), j]
                got(block, sem)
                if all_rows or n < 2:
                    put(block, block, sem, ahead[q], cond, lambda: dpg.at[0, piece(0)])

    pl.when(other)(lambda: pass_on(other, 1, True))
    pl.when(owner)(lambda: pass_on(owner, 2, True))

    for i in range(2):
        got(hg.at[i], h_r.at[i])

    def part_out(i):
        o = dot(hg[0], w2g[i, :384, :]) + dot(hg[1], w2g[i, 384:, :])
        return o.astype(BF)

    o = part_out(1 - k)
    for j in range(4):
        ys[0, j] = o[:, j * 128:(j + 1) * 128]
    put(ys.at[0], yx, yx_r, (z, col(y, x, 1 - k)))
    o = part_out(k)
    for j in range(4):
        ys[1, j] = o[:, j * 128:(j + 1) * 128]
    pl.when(other)(lambda: pass_on(other, 3, False))
    got(yx, yx_r)
    for j in range(4):
        ys[1, j] = ys[1, j] + yx[j]
    keep(ys.at[1, y], ya.at[y], y1_r.at[y])
    for i in (1, 3, 2):
        put(ys.at[1, (y + i) % 4], ya.at[y], y1_r.at[y], (z, col((y + i) % 4, x, k)))

    def part_w2(i, _):
        g = gg[i].reshape(384, 512)
        for r in range(2):
            o = t_dot(hg[r], g)
            for j in range(4):
                d2s[i, j, pl.ds(r * 384, 384), :] = o[:, j * 128:(j + 1) * 128].astype(BF)
        return 0

    lax.fori_loop(0, 2, part_w2, 0)
    for i in (2, 1, 3, 0):
        j = (y + i) % 4
        put(d2s.at[1 - k, j], d2x.at[j], d2x_r.at[j], (z, col(y, x, 1 - k)))

    @pl.when(owner)
    def _():
        for j in range(4):
            got(dpg.at[block_at(4), piece(j)], dp_r.at[block_at(4), j])

    for i in range(2):
        o = dot_t(dpg[0], w1g[0, pl.ds(i * 256, 256), :])
        for j in range(1, 4):
            o = o + dot_t(dpg[j], w1g[j, pl.ds(i * 256, 256), :])
        dxs[i] = o.astype(BF).reshape(2, 4, 48, 256)
    for i in range(4):
        for d in range(2):
            dx, dk = (x + i) % 4, (k + d) % 2
            if i or d:
                put(dxs.at[dk, :, dx], dxr.at[x, k], dx1_r.at[x, k], (z, col(y, dx, dk)))
            else:
                keep(dxs.at[dk, :, dx], dxr.at[x, k], dx1_r.at[x, k])

    far_y = (y + 2) % 4
    for i in (2, 1, 3, 0):
        got(d2x.at[(y + i) % 4], d2x_r.at[(y + i) % 4])
    put(d2s.at[k, far_y], d2t.at[0], d2t_r.at[0], (z, col(up, x, k)))
    put(d2x.at[far_y], d2t.at[1], d2t_r.at[1], (z, col(down, x, k)))
    put(d2x.at[up], d2r.at[0, 1], d2_r.at[0, 1], (z, col(up, x, k)))
    put(d2s.at[k, down], d2r.at[1, 0], d2_r.at[1, 0], (z, col(down, x, k)))

    def part_w1(i, _):
        for r in range(2):
            d1s[i, pl.ds(r * 256, 256), :] = t_dot(xg[r].reshape(384, 256), dpg[i]).astype(BF)
        total = jnp.sum(dpg[i].astype(F32), axis=0, keepdims=True)
        bs[i] = jnp.broadcast_to(total, (8, 384))
        return 0

    lax.fori_loop(0, 4, part_w1, 0)
    low, high = pl.ds(0, 256), pl.ds(256, 256)
    for d, (dy, rows) in enumerate(((up, low), (down, high))):
        put(d1s.at[(y + 2) % 4, rows], d1t.at[d], d1t_r.at[d], (z, col(dy, x, k)))
    for d, (dy, rows) in enumerate(((up, high), (down, low))):
        put(d1s.at[dy, rows], d1r.at[d, rows], d1_r.at[d, 0], (z, col(dy, x, k)))
    keep(bs.at[y], dbr.at[y], db_r.at[y])
    for i in (1, 3, 2):
        dy = (y + i) % 4
        put(bs.at[dy], dbr.at[y], db_r.at[y], (z, col(dy, x, k)))

    for i in range(4):
        got(ya.at[i], y1_r.at[i])
    for i in range(8):
        j = (z + i) % 8
        rows = pl.ds(pl.multiple_of(j % 2 * 192, 192), 192)
        if i:
            put(ya.at[j // 2, rows], yr.at[z], y2_r.at[z], (j, c))
        else:
            keep(ya.at[j // 2, rows], yr.at[z], y2_r.at[z])

    for d in range(2):
        got(d2t.at[d], d2t_r.at[d])
    d2s[k, up] = d2s[k, up] + d2t[0]
    put(d2s.at[k, up], d2r.at[0, 0], d2_r.at[0, 0], (z, col(up, x, k)))
    d2x[down] = d2x[down] + d2t[1]
    put(d2x.at[down], d2r.at[1, 1], d2_r.at[1, 1], (z, col(down, x, k)))

    for d, (dy, rows) in enumerate(((up, low), (down, high))):
        got(d1t.at[d], d1t_r.at[d])
        d1s[dy, rows, :] = d1s[dy, rows, :] + d1t[d]
        put(d1s.at[dy, rows], d1r.at[d, rows], d1_r.at[d, 1], (z, col(dy, x, k)))

    for i in range(4):
        for d in range(2):
            got(dxr.at[i, d], dx1_r.at[i, d])
    for h in range(2):
        o = dxr[0, 0, h].astype(F32)
        for j in range(1, 8):
            o = o + dxr[j // 2, j % 2, h].astype(F32)
        for d in range(2):
            dxb[h, d] = o[:, d * 128:(d + 1) * 128].astype(BF)
    for h in range(2):
        for d in range(2):
            dev = back[2 * h + d]
            put_any(
                dxb.at[h, d], ot.at[x], dx2_r.at[x], dev,
                jnp.logical_and(dev[0] == z, dev[1] == c),
            )

    for i in range(2):
        for d in range(2):
            got(d2r.at[i, d], d2_r.at[i, d])

    def sum_w2(i, _):
        rows = pl.ds(pl.multiple_of(i * 64, 64), 64)
        for d, local in enumerate((d2s.at[k, y], d2x.at[y])):
            o = local[rows, :].astype(F32)
            for j in range(2):
                o = o + d2r[j, d, rows, :].astype(F32)
            start = (k if d == 0 else 1 - k) * 768 + i * 64
            out_w2[pl.ds(pl.multiple_of(start, 64), 64), :] = o
        return 0

    lax.fori_loop(0, 12, sum_w2, 0)
    for i in range(8):
        got(yr.at[i], y2_r.at[i])
    o = yr[0].astype(F32)
    for j in range(1, 8):
        o = o + yr[j].astype(F32)
    out_y[...] = o.astype(BF)
    for i in range(4):
        got(ot.at[i], dx2_r.at[i])
    out_x[...] = ot[...].reshape(192, 128)
    for i in range(4):
        got(dbr.at[i], db_r.at[i])
    for d, rows in enumerate((high, low)):
        got(d1r.at[d, rows], d1_r.at[d, 0])
        rest = low if d == 0 else high
        got(d1r.at[d, rest], d1_r.at[d, 1])

    def sum_w1(i, _):
        rows = pl.ds(pl.multiple_of(i * 32, 32), 32)
        o = d1s[y, rows, :].astype(F32)
        for j in range(2):
            o = o + d1r[j, rows, :].astype(F32)
        out_w1[rows, :] = o
        return 0

    lax.fori_loop(0, 16, sum_w1, 0)
    o = dbr[0] + dbr[1] + dbr[2] + dbr[3]
    out_b[...] = o[:1]

    for i, (like, cond) in enumerate(sent):
        ref = like()
        wait = pltpu.make_async_copy(ref, ref, send.at[i]).wait
        if cond is None:
            wait()
        else:
            pl.when(cond)(wait)


SENDS = 220
DMA = pltpu.SemaphoreType.DMA


def per_device(tokens, w_in, bias_in, w_out, grad_out):
    vm = pltpu.VMEM
    spec = pl.BlockSpec(memory_space=pltpu.VMEM)
    shapes = [
        ((192, 128), BF), ((192, 128), BF), ((512, 384), F32), ((1, 384), F32), ((1536, 128), F32),
    ]
    out = pl.pallas_call(
        kernel,
        out_shape=[jax.ShapeDtypeStruct(s, d) for s, d in shapes],
        in_specs=[spec] * 5,
        out_specs=[spec] * 5,
        scratch_shapes=[
            vm((2, 48, 256), BF),
            vm((2, 2, 4, 48, 256), BF),
            vm((4, 512, 384), BF),
            vm((768, 128), BF),
            vm((2, 768, 512), BF),
            vm((8, 192, 128), BF),
            vm((2, 2, 192, 512), BF),
            vm((8, 384), F32),
            vm((4, 8, 384), F32),
            vm((4, 384, 384), BF),
            vm((2, 2, 384, 384), BF),
            vm((2, 2, 384, 384), BF),
            vm((2, 384, 384), BF),
            vm((4, 384, 384), BF),
            vm((384, 384), BF),
            vm((2, 384, 384), BF),
            vm((4, 384, 384), BF),
            vm((2, 4, 384, 128), BF),
            vm((4, 384, 128), BF),
            vm((4, 384, 128), BF),
            vm((8, 192, 128), BF),
            vm((2, 4, 768, 128), BF),
            vm((4, 768, 128), BF),
            vm((2, 768, 128), BF),
            vm((2, 2, 768, 128), BF),
            vm((2, 2, 4, 48, 256), BF),
            vm((4, 2, 2, 48, 256), BF),
            vm((2, 2, 48, 128), BF),
            vm((4, 48, 128), BF),
            vm((4, 512, 384), BF),
            vm((2, 256, 384), BF),
            vm((2, 512, 384), BF),
            vm((4, 8, 384), F32),
            vm((4, 8, 384), F32),
            DMA((SENDS,)),
            DMA((2, 2)), DMA((4, 2)), DMA((4, 2)), DMA, DMA, DMA((4, 2, 2)), DMA((4,)),
            DMA((8,)), DMA((4,)), DMA, DMA((2, 2, 4)), DMA((4,)), DMA((2,)), DMA((4, 4)),
            DMA, DMA((4,)), DMA((8,)), DMA((4,)), DMA((2,)), DMA((2, 2)), DMA((4, 2)), DMA((4,)),
            DMA((2,)), DMA((2, 2)), DMA((4,)),
        ],
        compiler_params=pltpu.CompilerParams(
            collective_id=0, has_side_effects=True, vmem_limit_bytes=56 * 2**20
        ),
        name="mlp_grad",
    )(tokens, w_in, bias_in.reshape(1, 384), w_out, grad_out)
    block_out, grad_tokens, grad_w_in, grad_bias, grad_w_out = out
    return block_out, grad_tokens, grad_w_in, grad_bias.reshape(384), grad_w_out


def solution(mesh):
    return jax.shard_map(
        per_device,
        mesh=mesh,
        in_specs=(P("row", "col"), P("row", "col"), P("col"), P("row", "col"), P("row", "col")),
        out_specs=(P("row", "col"), P("row", "col"), P("row", "col"), P("col"), P("row", "col")),
        check_vma=False,
    )
```

```python
import functools

import jax
import jax.numpy as jnp
from jax import lax
from jax.experimental import pallas as pl
from jax.experimental.pallas import tpu as pltpu
from jax.sharding import PartitionSpec as P

MESH = pl.DeviceIdType.MESH
BF, F32 = jnp.bfloat16, jnp.float32
S2PI = 0.7978845608028654
CUBIC = 0.044715


def dot(a, b):
    return lax.dot_general(a, b, (((1,), (0,)), ((), ())), preferred_element_type=F32)


def dot_t(a, b):
    return lax.dot_general(a, b, (((1,), (1,)), ((), ())), preferred_element_type=F32)


def t_dot(a, b):
    return lax.dot_general(a, b, (((0,), (0,)), ((), ())), preferred_element_type=F32)


def col(y, x, k):
    return y * 8 + x * 2 + k


def lanes(i, n):
    return pl.ds(pl.multiple_of(i * n, n), n)


def kernel(
    tok, w1, bias, w2, go,
    out_y, out_x, out_w1, out_b, out_w2,
    xa, xg, w1g, w2h, w2g, gs, gg, b8, bg,
    ps, rz, tz, dhs, dhr, ho, hg, dpg,
    ys, yx, ya, yr, d2s, d2x, d2t, d2r, dxs, dxr, dxb, ot, d1s, d1t, d1r, bs, dbr, r_y, r_w1, r_w2, r_b,
    send, x1_r, x2_r, w1_r, w2s_r, w2k_r, w2_r, b_r, g1_r, g2_r, g3_r, p_r, dh_r, h_r, dp_r,
    yx_r, y1_r, y2_r, d2x_r, d2t_r, d2_r, dx1_r, dx2_r, d1t_r, d1_r, db_r, out_r,
):
    z, c = lax.axis_index("row"), lax.axis_index("col")
    k, x, y = c % 2, (c // 2) % 4, c // 8
    sent = []

    def put(src, dst, rsem, dev, cond=None, like=None):
        copy = pltpu.make_async_remote_copy(
            src_ref=src, dst_ref=dst, send_sem=send.at[len(sent)], recv_sem=rsem,
            device_id=dev, device_id_type=MESH,
        )
        if cond is None or like is not None:
            copy.start()
        else:
            pl.when(cond)(copy.start)
        sent.append((like or (lambda: src), cond))

    def put_any(src, dst, rsem, dev, here):
        put(src, dst, rsem, dev, jnp.logical_not(here))
        pl.when(here)(pltpu.make_async_copy(src, dst, rsem).start)

    def keep(src, dst, rsem):
        pltpu.make_async_copy(src, dst, rsem).start()

    def got(dst, rsem):
        pltpu.make_async_copy(dst, dst, rsem).wait()

    barrier = pltpu.get_barrier_semaphore()
    near = [((z + i) % 8, c) for i in range(1, 8)]
    near += [(z, col((y + i) % 4, x, (k + d) % 2)) for i in range(4) for d in range(2) if i or d]
    near += [(z, col(y, (x + i) % 4, (k + d) % 2)) for i in range(1, 4) for d in range(2)]
    far = [(2 * y + x // 2, col(z // 2, j, x % 2)) for j in range(4)]
    back = [(2 * y + h, col(z // 2, 2 * (z % 2) + k, d)) for h in range(2) for d in range(2)]
    for dev in near + far + back:
        pl.semaphore_signal(barrier, inc=1, device_id=dev, device_id_type=MESH)
    pl.semaphore_wait(barrier, len(near + far + back))

    for j in range(4):
        here = jnp.logical_and(far[j][0] == z, far[j][1] == c)
        put_any(
            tok.at[pl.ds(j * 48, 48)], xa.at[z % 2, :, lanes(k, 128)], x1_r.at[z % 2, k], far[j], here
        )
    keep(go, gs.at[z], g1_r.at[z])
    for i in (4, 3, 5, 2, 6, 1, 7):
        put(go, gs.at[z], g1_r.at[z], ((z + i) % 8, c))
    up, down = (y + 1) % 4, (y + 3) % 4
    b8[...] = jnp.broadcast_to(bias[...].reshape(1, 384), b8.shape)
    for i in range(2):
        rows = pl.ds(i * 256, 256)
        keep(w1.at[rows], w1g.at[y, rows], w1_r.at[y, i])
    for i in range(2):
        for n, dy in enumerate((up, down)):
            rows = pl.ds((i ^ n) * 256, 256)
            put(w1.at[rows], w1g.at[y, rows], w1_r.at[y, i ^ n], (z, col(dy, x, k)))
    mine = pl.ds(pl.multiple_of(k * 768, 768), 768)
    theirs = pl.ds(pl.multiple_of((1 - k) * 768, 768), 768)
    put(w2.at[theirs], w2h, w2s_r, (z, col(y, x, 1 - k)))
    keep(w2.at[mine], w2g.at[k, :, lanes(y, 128)], w2k_r)
    keep(b8, bg.at[y], b_r.at[y])
    for i in (1, 2, 3):
        put(b8, bg.at[y], b_r.at[y], (z, col((y + i) % 4, x, k)))
    for h in range(2):
        for d in range(2):
            got(xa.at[h, :, pl.ds(d * 128, 128)], x1_r.at[h, d])
    keep(xa, xg.at[k, :, x], x2_r.at[x, k])
    for i in range(4):
        for d in range(2):
            if i or d:
                put(xa, xg.at[k, :, x], x2_r.at[x, k], (z, col(y, (x + i) % 4, (k + d) % 2)))

    for i, (dy, fy) in enumerate(((up, down), (down, up))):
        rows = pl.ds(i * 256, 256)
        got(w1g.at[fy, rows], w1_r.at[fy, i])
        put(w1g.at[fy, rows], w1g.at[fy, rows], w1_r.at[fy, i], (z, col(dy, x, k)))
    got(w2h, w2s_r)
    keep(w2h, w2g.at[1 - k, :, lanes(y, 128)], w2s_r)

    def start_w2(i):
        for dy in (up, down):
            rows = pl.ds(pl.multiple_of(k * 768 + i * 384, 384), 384)
            put(
                w2.at[rows], w2g.at[k, pl.ds(i * 384, 384), lanes(y, 128)], w2_r.at[y, k, i],
                (z, col(dy, x, k)),
            )
            rows = pl.ds(i * 384, 384)
            put(
                w2h.at[rows], w2g.at[1 - k, rows, lanes(y, 128)], w2_r.at[y, 1 - k, i],
                (z, col(dy, x, k)),
            )

    start_w2(0)

    def pass_w2(i):
        for d, (dy, fy) in enumerate(((up, down), (down, up))):
            block = w2g.at[d, pl.ds(i * 384, 384), lanes(fy, 128)]
            got(block, w2_r.at[fy, d, i])
            put(block, block, w2_r.at[fy, d, i], (z, col(dy, x, k)))

    for i in range(8):
        got(gs.at[i], g1_r.at[i])
    for i in (2, 1, 3, 0):
        dy = (y + i) % 4
        src, dst = gs.at[pl.ds(2 * dy, 2)], gg.at[k, :, :, lanes(y, 128)]
        if i:
            put(src, dst, g2_r.at[y], (z, col(dy, x, k)))
        else:
            keep(src, dst, g2_r.at[y])

    for i in range(4):
        for d in range(2):
            got(xg.at[d, :, i], x2_r.at[i, d])
    got(w1g.at[y, pl.ds(0, 256)], w1_r.at[y, 0])
    got(w1g.at[y, pl.ds(256, 256)], w1_r.at[y, 1])
    got(w1g.at[down, pl.ds(256, 256)], w1_r.at[down, 1])
    got(w1g.at[up, pl.ds(0, 256)], w1_r.at[up, 0])
    for i in range(2):
        got(w1g.at[(y + 2) % 4, pl.ds(i * 256, 256)], w1_r.at[(y + 2) % 4, i])

    owner = z % 2 == x // 2
    other = jnp.logical_not(owner)
    odd = (z + x // 2) % 2
    ways = ((1, 0), (-1, 1))
    ahead = [((z + 1) % 8, c), ((z + 7) % 8, c)]

    def block_at(step):
        return ((z + step + 16) % 8) // 2

    first = [block_at(s * (4 - odd)) for s, _ in ways]
    second = [block_at(s * (2 - odd)) for s, _ in ways]

    def piece(j):
        return pl.ds(j * 96, 96)

    def halves(q):
        return (2, 3, 0, 1) if q else (0, 1, 2, 3)

    def part(i, _):
        x0 = xg[0].reshape(384, 256)
        x1 = xg[1].reshape(384, 256)
        ps[i] = (dot(x0, w1g[i, :256]) + dot(x1, w1g[i, 256:])).astype(BF)
        return 0

    lax.fori_loop(0, 4, part, 0)
    for n in range(2):
        for _, q in ways:
            for cond, j in ((owner, halves(q)[n]), (other, halves(q)[2 + n])):
                put(
                    ps.at[first[q], piece(j)], rz.at[q, 0, piece(j)], p_r.at[q, 0, j],
                    ahead[q], cond,
                )
    home = 2 * (z % 2) + k

    def part_hidden(i):
        for d in range(2):
            for j in (down if d else up, (y + 2) % 4):
                got(w2g.at[d, pl.ds(i * 384, 384), lanes(j, 128)], w2_r.at[j, d, i])
        rows = pl.ds(i * 384, 384)
        g0 = gg[0].reshape(384, 512)
        g1 = gg[1].reshape(384, 512)
        dhs[i] = (dot_t(g0, w2g[0, rows, :]) + dot_t(g1, w2g[1, rows, :])).astype(BF)
        put_any(
            dhs.at[i], dhr.at[x], dh_r.at[x], (z, col(y, home, i)),
            jnp.logical_and(home == x, k == i),
        )

    def relay(cond, mine, kind, to, n, q):
        j = (halves(q) if kind == to == 0 else halves(1 - q))[n]
        got(rz.at[q, kind, piece(j)], p_r.at[q, kind, j])
        tz[q, to, piece(j), :] = ps[mine, piece(j), :] + rz[q, kind, piece(j), :]
        put(
            tz.at[q, to, piece(j)], rz.at[q, to, piece(j)], p_r.at[q, to, j], ahead[q], cond,
            lambda: tz.at[q, to, piece(j)],
        )

    for i in range(4):
        got(gg.at[k, :, :, pl.ds(i * 128, 128)], g2_r.at[i])
    put(gg.at[k], gg.at[k], g3_r, (z, col(y, x, 1 - k)))

    pass_w2(0)
    start_w2(1)

    @pl.when(other)
    def _():
        for n in range(2):
            for _, q in ways:
                relay(other, first[q], 0, 0, n, q)

    @pl.when(owner)
    def _():
        for n in range(2):
            for _, q in ways:
                relay(owner, second[q], 0, 1, n, q)

    got(gg.at[1 - k], g3_r)
    got(w2g.at[k, :, lanes(y, 128)], w2k_r)
    got(w2g.at[1 - k, :, lanes(y, 128)], w2s_r)
    part_hidden(0)

    @pl.when(owner)
    def _():
        for n in range(2, 4):
            for _, q in ways:
                relay(owner, second[q], 0, 1, n, q)

    pass_w2(1)

    @pl.when(other)
    def _():
        for n in range(4):
            for _, q in ways:
                relay(other, second[q], 1, 1, n, q)

    part_hidden(1)

    @pl.when(owner)
    def _():
        for i in range(4):
            got(bg.at[i], b_r.at[i])
        for j in range(4):
            for _, q in ways:
                got(rz.at[q, 1, piece(j)], p_r.at[q, 1, j])
        for i in range(4):
            got(dhr.at[i], dh_r.at[i])

        def point(i, _):
            rows = pl.ds(pl.multiple_of(i * 16, 16), 16)
            v = jnp.broadcast_to(bg[z // 2, pl.ds(0, 1), :], (16, 384))
            v = v + ps[z // 2, rows, :].astype(F32)
            v = v + (rz[0, 1, rows, :].astype(F32) + rz[1, 1, rows, :].astype(F32))
            grad = dhr[0, rows, :].astype(F32)
            for j in range(1, 4):
                grad = grad + dhr[j, rows, :].astype(F32)
            v2 = v * v
            t = jnp.tanh(S2PI * (v + CUBIC * (v2 * v)))
            cdf = 0.5 * (1.0 + t)
            ho[rows, :] = (v * cdf).astype(BF)
            slope = cdf + (0.5 * v) * (1.0 - t * t) * (S2PI * (1.0 + 3.0 * CUBIC * v2))
            dpg[z // 2, rows, :] = (grad * slope).astype(BF)
            return 0

        lax.fori_loop(0, 24, point, 0)
        for n in range(4):
            for _, q in ways:
                block = dpg.at[z // 2, piece(halves(q)[n])]
                put(block, block, dp_r.at[z // 2, halves(q)[n]], ahead[q], owner, lambda: dpg.at[0, piece(0)])

    @pl.when(jnp.logical_not(owner))
    def _():
        for i in range(4):
            got(bg.at[i], b_r.at[i])

    for i in range(4):
        here = jnp.logical_and((x + i) % 4 == x, x % 2 == k)
        put(
            ho, hg.at[k], h_r.at[k], (z, col(y, (x + i) % 4, x % 2)),
            jnp.logical_and(owner, jnp.logical_not(here)),
        )
        pl.when(jnp.logical_and(owner, here))(
            pltpu.make_async_copy(ho, hg.at[k], h_r.at[k]).start
        )

    low, high = pl.ds(0, 256), pl.ds(256, 256)
    w1_key = len(sent)
    for rows in (low, high, high, low):
        sent.append((lambda: d1t.at[0], None))

    def part_w1(step):
        b = block_at(step)
        for r in range(2):
            d1s[b, pl.ds(r * 256, 256), :] = t_dot(xg[r].reshape(384, 256), dpg[b]).astype(BF)
        total = jnp.sum(dpg[b].astype(F32), axis=0, keepdims=True)
        bs[b] = jnp.broadcast_to(total, (8, 384))
        off = (b - y + 4) % 4

        def go_on(key, rows, dst, sem, dy):
            pltpu.make_async_remote_copy(
                src_ref=d1s.at[b, rows], dst_ref=dst, send_sem=send.at[w1_key + key], recv_sem=sem,
                device_id=(z, col(dy, x, k)), device_id_type=MESH,
            ).start()

        @pl.when(off == 2)
        def _():
            go_on(0, low, d1t.at[0], d1t_r.at[0], up)
            go_on(1, high, d1t.at[1], d1t_r.at[1], down)

        @pl.when(off == 1)
        def _():
            go_on(2, high, d1r.at[0, high], d1_r.at[0, 0], up)

        @pl.when(off == 3)
        def _():
            go_on(3, low, d1r.at[1, low], d1_r.at[1, 0], down)

    def pass_on(cond, back_by, all_rows):
        for n in range(4):
            for s, q in ways:
                j = halves(q)[n]
                block = dpg.at[block_at(-s * back_by), piece(j)]
                sem = dp_r.at[block_at(-s * back_by), j]
                got(block, sem)
                if all_rows or n < 2:
                    put(block, block, sem, ahead[q], cond, lambda: dpg.at[0, piece(0)])

    @pl.when(other)
    def _():
        pass_on(other, 1, True)
        part_w1(1)
        part_w1(-1)

    @pl.when(owner)
    def _():
        part_w1(0)
        pass_on(owner, 2, True)
        part_w1(2)
        part_w1(-2)

    pl.when(other)(lambda: pass_on(other, 3, False))

    for i in range(2):
        got(hg.at[i], h_r.at[i])

    def part_out(i, slot):
        o = dot(hg[0], w2g[i, :384, :]) + dot(hg[1], w2g[i, 384:, :])
        for j in range(4):
            ys[slot, j] = o[:, j * 128:(j + 1) * 128].astype(BF)

    def part_w2(i):
        g = gg[i].reshape(384, 512)
        for r in range(2):
            o = t_dot(hg[r], g)
            for j in range(4):
                d2s[i, j, pl.ds(r * 384, 384), :] = o[:, j * 128:(j + 1) * 128].astype(BF)

    part_w2(1 - k)
    for i in (2, 1, 3, 0):
        j = (y + i) % 4
        put(d2s.at[1 - k, j], d2x.at[j], d2x_r.at[j], (z, col(y, x, 1 - k)))
    part_out(1 - k, 0)
    put(ys.at[0], yx, yx_r, (z, col(y, x, 1 - k)))
    part_w2(k)
    far_y = (y + 2) % 4
    put(d2s.at[k, far_y], d2t.at[0], d2t_r.at[0], (z, col(up, x, k)))
    got(d2x.at[far_y], d2x_r.at[far_y])
    put(d2x.at[far_y], d2t.at[1], d2t_r.at[1], (z, col(down, x, k)))
    part_out(k, 1)
    got(yx, yx_r)
    for j in range(4):
        ys[1, j] = ys[1, j] + yx[j]
    keep(ys.at[1, y], ya.at[y], y1_r.at[y])
    for i in (1, 3, 2):
        put(ys.at[1, (y + i) % 4], ya.at[y], y1_r.at[y], (z, col((y + i) % 4, x, k)))
    for i in (1, 3, 0):
        got(d2x.at[(y + i) % 4], d2x_r.at[(y + i) % 4])
    put(d2x.at[up], d2r.at[0, 1], d2_r.at[0, 1], (z, col(up, x, k)))
    put(d2s.at[k, down], d2r.at[1, 0], d2_r.at[1, 0], (z, col(down, x, k)))

    @pl.when(owner)
    def _():
        for j in range(4):
            got(dpg.at[block_at(4), piece(j)], dp_r.at[block_at(4), j])

    for i in range(2):
        o = dot_t(dpg[0], w1g[0, pl.ds(i * 256, 256), :])
        for j in range(1, 4):
            o = o + dot_t(dpg[j], w1g[j, pl.ds(i * 256, 256), :])
        dxs[i] = o.astype(BF).reshape(2, 4, 48, 256)
    for i in range(4):
        for d in range(2):
            dx, dk = (x + i) % 4, (k + d) % 2
            if i or d:
                put(dxs.at[dk, :, dx], dxr.at[x, k], dx1_r.at[x, k], (z, col(y, dx, dk)))
            else:
                keep(dxs.at[dk, :, dx], dxr.at[x, k], dx1_r.at[x, k])

    @pl.when(owner)
    def _():
        part_w1(4)

    @pl.when(other)
    def _():
        part_w1(3)
        part_w1(-3)

    keep(bs.at[y], dbr.at[y], db_r.at[y])
    for i in (1, 3, 2):
        dy = (y + i) % 4
        put(bs.at[dy], dbr.at[y], db_r.at[y], (z, col(dy, x, k)))

    for i in range(4):
        got(ya.at[i], y1_r.at[i])
    for i in range(8):
        j = (z + i) % 8
        rows = pl.ds(pl.multiple_of(j % 2 * 192, 192), 192)
        if i:
            put(ya.at[j // 2, rows], yr.at[z], y2_r.at[z], (j, c))
        else:
            keep(ya.at[j // 2, rows], yr.at[z], y2_r.at[z])

    for i in range(4):
        for d in range(2):
            got(dxr.at[i, d], dx1_r.at[i, d])
    for h in range(2):
        o = dxr[0, 0, h].astype(F32)
        for j in range(1, 8):
            o = o + dxr[j // 2, j % 2, h].astype(F32)
        for d in range(2):
            dxb[h, d] = o[:, d * 128:(d + 1) * 128].astype(BF)
    for h in range(2):
        for d in range(2):
            dev = back[2 * h + d]
            put_any(
                dxb.at[h, d], ot.at[lanes(x, 48)], dx2_r.at[x], dev,
                jnp.logical_and(dev[0] == z, dev[1] == c),
            )

    for d in range(2):
        got(d2t.at[d], d2t_r.at[d])
    d2s[k, up] = d2s[k, up] + d2t[0]
    put(d2s.at[k, up], d2r.at[0, 0], d2_r.at[0, 0], (z, col(up, x, k)))
    d2x[down] = d2x[down] + d2t[1]
    put(d2x.at[down], d2r.at[1, 1], d2_r.at[1, 1], (z, col(down, x, k)))

    for d, (dy, rows) in enumerate(((up, low), (down, high))):
        got(d1t.at[d], d1t_r.at[d])
        d1s[dy, rows, :] = d1s[dy, rows, :] + d1t[d]
        put(d1s.at[dy, rows], d1r.at[d, rows], d1_r.at[d, 1], (z, col(dy, x, k)))

    for i in range(2):
        for d in range(2):
            got(d2r.at[i, d], d2_r.at[i, d])

    def sum_w2(i, _):
        rows = pl.ds(pl.multiple_of(i * 64, 64), 64)
        for d, local in enumerate((d2s.at[k, y], d2x.at[y])):
            o = local[rows, :].astype(F32)
            for j in range(2):
                o = o + d2r[j, d, rows, :].astype(F32)
            start = (k if d == 0 else 1 - k) * 768 + i * 64
            r_w2[pl.ds(pl.multiple_of(start, 64), 64), :] = o
        return 0

    lax.fori_loop(0, 12, sum_w2, 0)
    keep(r_w2, out_w2, out_r.at[0])
    for i in range(8):
        got(yr.at[i], y2_r.at[i])
    o = yr[0].astype(F32)
    for j in range(1, 8):
        o = o + yr[j].astype(F32)
    r_y[...] = o.astype(BF)
    keep(r_y, out_y, out_r.at[1])
    for i in range(4):
        got(ot.at[pl.ds(i * 48, 48)], dx2_r.at[i])
    keep(ot, out_x, out_r.at[2])
    for i in range(4):
        got(dbr.at[i], db_r.at[i])
    for d, rows in enumerate((high, low)):
        got(d1r.at[d, rows], d1_r.at[d, 0])
        rest = low if d == 0 else high
        got(d1r.at[d, rest], d1_r.at[d, 1])

    def sum_w1(i, _):
        rows = pl.ds(pl.multiple_of(i * 32, 32), 32)
        o = d1s[y, rows, :].astype(F32)
        for j in range(2):
            o = o + d1r[j, rows, :].astype(F32)
        r_w1[rows, :] = o
        return 0

    lax.fori_loop(0, 16, sum_w1, 0)
    keep(r_w1, out_w1, out_r.at[3])
    r_b[...] = dbr[0] + dbr[1] + dbr[2] + dbr[3]
    keep(r_b, out_b, out_r.at[4])
    for i, ref in enumerate((out_w2, out_y, out_x, out_w1, out_b)):
        got(ref, out_r.at[i])

    for i, (like, cond) in enumerate(sent):
        ref = like()
        wait = pltpu.make_async_copy(ref, ref, send.at[i]).wait
        if cond is None:
            wait()
        else:
            pl.when(cond)(wait)


def hand_over(*refs):
    stage, sems = refs[10:14], refs[14]
    parts = []
    for n, i in enumerate((2, 4, 0, 1)):
        rows = refs[i].shape[0] // 2
        for half in range(2):
            at = pl.ds(half * rows, rows)
            key = 2 * n + half
            parts.append((
                pltpu.make_async_copy(refs[i].at[at], stage[n].at[at], sems.at[0, key]),
                pltpu.make_async_copy(stage[n].at[at], refs[5 + i].at[at], sems.at[1, key]),
            ))
    for into, _ in parts:
        into.start()
    refs[8][...] = refs[3][0]
    for into, away in parts:
        into.wait()
        away.start()
    for _, away in parts:
        away.wait()


SENDS = 220
DMA = pltpu.SemaphoreType.DMA


def per_device(tokens, w_in, bias_in, w_out, grad_out):
    vm = pltpu.VMEM
    spec = pl.BlockSpec(memory_space=pltpu.VMEM)
    away = pl.BlockSpec(memory_space=pl.ANY)
    shapes = [
        ((192, 128), BF), ((192, 128), BF), ((512, 384), F32), ((8, 384), F32), ((1536, 128), F32),
    ]
    out = pl.pallas_call(
        kernel,
        out_shape=[jax.ShapeDtypeStruct(s, d) for s, d in shapes],
        in_specs=[away, away, spec, away, away],
        out_specs=[away] * 5,
        scratch_shapes=[
            vm((2, 48, 256), BF),
            vm((2, 2, 4, 48, 256), BF),
            vm((4, 512, 384), BF),
            vm((768, 128), BF),
            vm((2, 768, 512), BF),
            vm((8, 192, 128), BF),
            vm((2, 2, 192, 512), BF),
            vm((8, 384), F32),
            vm((4, 8, 384), F32),
            vm((4, 384, 384), BF),
            vm((2, 2, 384, 384), BF),
            vm((2, 2, 384, 384), BF),
            vm((2, 384, 384), BF),
            vm((4, 384, 384), BF),
            vm((384, 384), BF),
            vm((2, 384, 384), BF),
            vm((4, 384, 384), BF),
            vm((2, 4, 384, 128), BF),
            vm((4, 384, 128), BF),
            vm((4, 384, 128), BF),
            vm((8, 192, 128), BF),
            vm((2, 4, 768, 128), BF),
            vm((4, 768, 128), BF),
            vm((2, 768, 128), BF),
            vm((2, 2, 768, 128), BF),
            vm((2, 2, 4, 48, 256), BF),
            vm((4, 2, 2, 48, 256), BF),
            vm((2, 2, 48, 128), BF),
            vm((192, 128), BF),
            vm((4, 512, 384), BF),
            vm((2, 256, 384), BF),
            vm((2, 512, 384), BF),
            vm((4, 8, 384), F32),
            vm((4, 8, 384), F32),
            vm((192, 128), BF),
            vm((512, 384), F32),
            vm((1536, 128), F32),
            vm((8, 384), F32),
            DMA((SENDS,)),
            DMA((2, 2)), DMA((4, 2)), DMA((4, 2)), DMA, DMA, DMA((4, 2, 2)), DMA((4,)),
            DMA((8,)), DMA((4,)), DMA, DMA((2, 2, 4)), DMA((4,)), DMA((2,)), DMA((4, 4)),
            DMA, DMA((4,)), DMA((8,)), DMA((4,)), DMA((2,)), DMA((2, 2)), DMA((4, 2)), DMA((4,)),
            DMA((2,)), DMA((2, 2)), DMA((4,)), DMA((5,)),
        ],
        compiler_params=pltpu.CompilerParams(
            collective_id=0, has_side_effects=True, vmem_limit_bytes=56 * 2**20
        ),
        name="mlp_grad",
    )(tokens, w_in, bias_in, w_out, grad_out)
    final = [s if i != 3 else ((384,), F32) for i, s in enumerate(shapes)]
    places = [spec if i == 3 else away for i in range(5)]
    return tuple(
        pl.pallas_call(
            hand_over,
            out_shape=[jax.ShapeDtypeStruct(s, d) for s, d in final],
            in_specs=places,
            out_specs=places,
            scratch_shapes=[vm(*shapes[i]) for i in (2, 4, 0, 1)] + [DMA((2, 8))],
            name="hand_over",
        )(*out)
    )


def solution(mesh):
    return jax.shard_map(
        per_device,
        mesh=mesh,
        in_specs=(P("row", "col"), P("row", "col"), P("col"), P("row", "col"), P("row", "col")),
        out_specs=(P("row", "col"), P("row", "col"), P("row", "col"), P("col"), P("row", "col")),
        check_vma=False,
    )
```

```python
import functools

import jax
import jax.numpy as jnp
from jax import lax
from jax.experimental import pallas as pl
from jax.experimental.pallas import tpu as pltpu
from jax.sharding import PartitionSpec as P

MESH = pl.DeviceIdType.MESH
BF, F32 = jnp.bfloat16, jnp.float32
S2PI = 0.7978845608028654
CUBIC = 0.044715


def dot(a, b):
    return lax.dot_general(a, b, (((1,), (0,)), ((), ())), preferred_element_type=F32)


def dot_t(a, b):
    return lax.dot_general(a, b, (((1,), (1,)), ((), ())), preferred_element_type=F32)


def t_dot(a, b):
    return lax.dot_general(a, b, (((0,), (0,)), ((), ())), preferred_element_type=F32)


def col(y, x, k):
    return y * 8 + x * 2 + k


def lanes(i, n):
    return pl.ds(pl.multiple_of(i * n, n), n)


def kernel(
    tok, w1, bias, w2, go,
    out_y, out_x, out_w1, out_b, out_w2,
    xa, xg, w1g, w2h, w2g, gs, gg, b8, bg,
    ps, rz, tz, dhs, dhr, ho, hg, dpg,
    ys, yx, ya, yr, d2s, d2x, d2t, d2r, dxs, dxr, dxb, ot, d1s, d1t, d1r, bs, dbr, r_y, r_w1, r_w2, r_b,
    send, x1_r, x2_r, w1_r, w2s_r, w2k_r, w2_r, b_r, g1_r, g2_r, g3_r, p_r, dh_r, h_r, dp_r,
    yx_r, y1_r, y2_r, d2x_r, d2t_r, d2_r, dx1_r, dx2_r, d1t_r, d1_r, db_r, out_r,
):
    z, c = lax.axis_index("row"), lax.axis_index("col")
    k, x, y = c % 2, (c // 2) % 4, c // 8
    sent = []

    def put(src, dst, rsem, dev, cond=None, like=None):
        copy = pltpu.make_async_remote_copy(
            src_ref=src, dst_ref=dst, send_sem=send.at[len(sent)], recv_sem=rsem,
            device_id=dev, device_id_type=MESH,
        )
        if cond is None or like is not None:
            copy.start()
        else:
            pl.when(cond)(copy.start)
        sent.append((like or (lambda: src), cond))

    def put_any(src, dst, rsem, dev, here):
        put(src, dst, rsem, dev, jnp.logical_not(here))
        pl.when(here)(pltpu.make_async_copy(src, dst, rsem).start)

    def keep(src, dst, rsem):
        pltpu.make_async_copy(src, dst, rsem).start()

    def got(dst, rsem):
        pltpu.make_async_copy(dst, dst, rsem).wait()

    barrier = pltpu.get_barrier_semaphore()
    near = [((z + i) % 8, c) for i in range(1, 8)]
    near += [(z, col((y + i) % 4, x, (k + d) % 2)) for i in range(4) for d in range(2) if i or d]
    near += [(z, col(y, (x + i) % 4, (k + d) % 2)) for i in range(1, 4) for d in range(2)]
    far = [(2 * y + x // 2, col(z // 2, j, x % 2)) for j in range(4)]
    back = [(2 * y + h, col(z // 2, 2 * (z % 2) + k, d)) for h in range(2) for d in range(2)]
    for dev in near + far + back:
        pl.semaphore_signal(barrier, inc=1, device_id=dev, device_id_type=MESH)
    pl.semaphore_wait(barrier, len(near + far + back))

    for j in range(4):
        here = jnp.logical_and(far[j][0] == z, far[j][1] == c)
        put_any(
            tok.at[pl.ds(j * 48, 48)], xa.at[z % 2, :, lanes(k, 128)], x1_r.at[z % 2, k], far[j], here
        )
    keep(go, gs.at[z], g1_r.at[z])
    for i in (4, 3, 5, 2, 6, 1, 7):
        put(go, gs.at[z], g1_r.at[z], ((z + i) % 8, c))
    up, down = (y + 1) % 4, (y + 3) % 4
    b8[...] = jnp.broadcast_to(bias[...].reshape(1, 384), b8.shape)
    for i in range(2):
        rows = pl.ds(i * 256, 256)
        keep(w1.at[rows], w1g.at[y, rows], w1_r.at[y, i])
    for i in range(2):
        for n, dy in enumerate((up, down)):
            rows = pl.ds((i ^ n) * 256, 256)
            put(w1.at[rows], w1g.at[y, rows], w1_r.at[y, i ^ n], (z, col(dy, x, k)))
    mine = pl.ds(pl.multiple_of(k * 768, 768), 768)
    theirs = pl.ds(pl.multiple_of((1 - k) * 768, 768), 768)
    put(w2.at[theirs], w2h, w2s_r, (z, col(y, x, 1 - k)))
    keep(w2.at[mine], w2g.at[k, :, lanes(y, 128)], w2k_r)
    keep(b8, bg.at[y], b_r.at[y])
    for i in (1, 2, 3):
        put(b8, bg.at[y], b_r.at[y], (z, col((y + i) % 4, x, k)))
    for h in range(2):
        for d in range(2):
            got(xa.at[h, :, pl.ds(d * 128, 128)], x1_r.at[h, d])
    keep(xa, xg.at[k, :, x], x2_r.at[x, k])
    for i in range(4):
        for d in range(2):
            if i or d:
                put(xa, xg.at[k, :, x], x2_r.at[x, k], (z, col(y, (x + i) % 4, (k + d) % 2)))

    for i, (dy, fy) in enumerate(((up, down), (down, up))):
        rows = pl.ds(i * 256, 256)
        got(w1g.at[fy, rows], w1_r.at[fy, i])
        put(w1g.at[fy, rows], w1g.at[fy, rows], w1_r.at[fy, i], (z, col(dy, x, k)))
    got(w2h, w2s_r)
    keep(w2h, w2g.at[1 - k, :, lanes(y, 128)], w2s_r)

    def start_w2(i):
        for dy in (up, down):
            rows = pl.ds(pl.multiple_of(k * 768 + i * 384, 384), 384)
            put(
                w2.at[rows], w2g.at[k, pl.ds(i * 384, 384), lanes(y, 128)], w2_r.at[y, k, i],
                (z, col(dy, x, k)),
            )
            rows = pl.ds(i * 384, 384)
            put(
                w2h.at[rows], w2g.at[1 - k, rows, lanes(y, 128)], w2_r.at[y, 1 - k, i],
                (z, col(dy, x, k)),
            )

    start_w2(0)

    def pass_w2(i):
        for d, (dy, fy) in enumerate(((up, down), (down, up))):
            block = w2g.at[d, pl.ds(i * 384, 384), lanes(fy, 128)]
            got(block, w2_r.at[fy, d, i])
            put(block, block, w2_r.at[fy, d, i], (z, col(dy, x, k)))

    for i in range(8):
        got(gs.at[i], g1_r.at[i])
    for i in (2, 1, 3, 0):
        dy = (y + i) % 4
        src, dst = gs.at[pl.ds(2 * dy, 2)], gg.at[k, :, :, lanes(y, 128)]
        if i:
            put(src, dst, g2_r.at[y], (z, col(dy, x, k)))
        else:
            keep(src, dst, g2_r.at[y])

    for i in range(4):
        for d in range(2):
            got(xg.at[d, :, i], x2_r.at[i, d])
    got(w1g.at[y, pl.ds(0, 256)], w1_r.at[y, 0])
    got(w1g.at[y, pl.ds(256, 256)], w1_r.at[y, 1])
    got(w1g.at[down, pl.ds(256, 256)], w1_r.at[down, 1])
    got(w1g.at[up, pl.ds(0, 256)], w1_r.at[up, 0])
    for i in range(2):
        got(w1g.at[(y + 2) % 4, pl.ds(i * 256, 256)], w1_r.at[(y + 2) % 4, i])

    owner = z % 2 == x // 2
    other = jnp.logical_not(owner)
    odd = (z + x // 2) % 2
    ways = ((1, 0), (-1, 1))
    ahead = [((z + 1) % 8, c), ((z + 7) % 8, c)]

    def block_at(step):
        return ((z + step + 16) % 8) // 2

    first = [block_at(s * (4 - odd)) for s, _ in ways]
    second = [block_at(s * (2 - odd)) for s, _ in ways]

    def piece(j):
        return pl.ds(j * 96, 96)

    def halves(q):
        return (2, 3, 0, 1) if q else (0, 1, 2, 3)

    def part(i, _):
        x0 = xg[0].reshape(384, 256)
        x1 = xg[1].reshape(384, 256)
        ps[i] = (dot(x0, w1g[i, :256]) + dot(x1, w1g[i, 256:])).astype(BF)
        return 0

    lax.fori_loop(0, 4, part, 0)
    for n in range(2):
        for _, q in ways:
            for cond, j in ((owner, halves(q)[n]), (other, halves(q)[2 + n])):
                put(
                    ps.at[first[q], piece(j)], rz.at[q, 0, piece(j)], p_r.at[q, 0, j],
                    ahead[q], cond,
                )
    home = 2 * (z % 2) + k

    def part_hidden(i):
        for d in range(2):
            for j in (down if d else up, (y + 2) % 4):
                got(w2g.at[d, pl.ds(i * 384, 384), lanes(j, 128)], w2_r.at[j, d, i])
        rows = pl.ds(i * 384, 384)
        g0 = gg[0].reshape(384, 512)
        g1 = gg[1].reshape(384, 512)
        dhs[i] = (dot_t(g0, w2g[0, rows, :]) + dot_t(g1, w2g[1, rows, :])).astype(BF)
        put_any(
            dhs.at[i], dhr.at[x], dh_r.at[x], (z, col(y, home, i)),
            jnp.logical_and(home == x, k == i),
        )

    def relay(cond, mine, kind, to, n, q):
        j = (halves(q) if kind == to == 0 else halves(1 - q))[n]
        got(rz.at[q, kind, piece(j)], p_r.at[q, kind, j])
        tz[q, to, piece(j), :] = ps[mine, piece(j), :] + rz[q, kind, piece(j), :]
        put(
            tz.at[q, to, piece(j)], rz.at[q, to, piece(j)], p_r.at[q, to, j], ahead[q], cond,
            lambda: tz.at[q, to, piece(j)],
        )

    for i in range(4):
        got(gg.at[k, :, :, pl.ds(i * 128, 128)], g2_r.at[i])
    put(gg.at[k], gg.at[k], g3_r, (z, col(y, x, 1 - k)))

    pass_w2(0)
    start_w2(1)

    @pl.when(other)
    def _():
        for n in range(2):
            for _, q in ways:
                relay(other, first[q], 0, 0, n, q)

    @pl.when(owner)
    def _():
        for n in range(2):
            for _, q in ways:
                relay(owner, second[q], 0, 1, n, q)

    got(gg.at[1 - k], g3_r)
    got(w2g.at[k, :, lanes(y, 128)], w2k_r)
    got(w2g.at[1 - k, :, lanes(y, 128)], w2s_r)
    part_hidden(0)

    @pl.when(owner)
    def _():
        for n in range(2, 4):
            for _, q in ways:
                relay(owner, second[q], 0, 1, n, q)

    pass_w2(1)

    @pl.when(other)
    def _():
        for n in range(4):
            for _, q in ways:
                relay(other, second[q], 1, 1, n, q)

    part_hidden(1)

    @pl.when(owner)
    def _():
        for i in range(4):
            got(bg.at[i], b_r.at[i])
        for j in range(4):
            for _, q in ways:
                got(rz.at[q, 1, piece(j)], p_r.at[q, 1, j])
        for i in range(4):
            got(dhr.at[i], dh_r.at[i])

        def point(i, _):
            rows = pl.ds(pl.multiple_of(i * 16, 16), 16)
            v = jnp.broadcast_to(bg[z // 2, pl.ds(0, 1), :], (16, 384))
            v = v + ps[z // 2, rows, :].astype(F32)
            v = v + (rz[0, 1, rows, :].astype(F32) + rz[1, 1, rows, :].astype(F32))
            grad = dhr[0, rows, :].astype(F32)
            for j in range(1, 4):
                grad = grad + dhr[j, rows, :].astype(F32)
            v2 = v * v
            t = jnp.tanh(S2PI * (v + CUBIC * (v2 * v)))
            cdf = 0.5 * (1.0 + t)
            ho[rows, :] = (v * cdf).astype(BF)
            slope = cdf + (0.5 * v) * (1.0 - t * t) * (S2PI * (1.0 + 3.0 * CUBIC * v2))
            dpg[z // 2, rows, :] = (grad * slope).astype(BF)
            return 0

        lax.fori_loop(0, 24, point, 0)
        for n in range(4):
            for _, q in ways:
                block = dpg.at[z // 2, piece(halves(q)[n])]
                put(block, block, dp_r.at[z // 2, halves(q)[n]], ahead[q], owner, lambda: dpg.at[0, piece(0)])

    @pl.when(jnp.logical_not(owner))
    def _():
        for i in range(4):
            got(bg.at[i], b_r.at[i])

    for i in range(4):
        here = jnp.logical_and((x + i) % 4 == x, x % 2 == k)
        put(
            ho, hg.at[k], h_r.at[k], (z, col(y, (x + i) % 4, x % 2)),
            jnp.logical_and(owner, jnp.logical_not(here)),
        )
        pl.when(jnp.logical_and(owner, here))(
            pltpu.make_async_copy(ho, hg.at[k], h_r.at[k]).start
        )

    far_y = (y + 2) % 4

    def half_rows(r):
        return pl.ds(r * 384, 384)

    def part_w2(i, r):
        o = t_dot(hg[r], gg[i].reshape(384, 512))
        for j in range(4):
            d2s[i, j, half_rows(r), :] = o[:, j * 128:(j + 1) * 128].astype(BF)

    def swap_w2(r):
        for i in (2, 1, 3, 0):
            j = (y + i) % 4
            put(
                d2s.at[1 - k, j, half_rows(r)], d2x.at[j, half_rows(r)], d2x_r.at[r, j],
                (z, col(y, x, 1 - k)),
            )

    def hop_one_w2(r):
        at = half_rows(r)
        for i in (2, 1, 3, 0):
            got(d2x.at[(y + i) % 4, at], d2x_r.at[r, (y + i) % 4])
        put(d2s.at[k, far_y, at], d2t.at[0, at], d2t_r.at[r, 0], (z, col(up, x, k)))
        put(d2x.at[far_y, at], d2t.at[1, at], d2t_r.at[r, 1], (z, col(down, x, k)))
        put(d2x.at[up, at], d2r.at[0, 1, at], d2_r.at[r, 0, 1], (z, col(up, x, k)))
        put(d2s.at[k, down, at], d2r.at[1, 0, at], d2_r.at[r, 1, 0], (z, col(down, x, k)))

    def hop_two_w2(r):
        at = half_rows(r)
        for d in range(2):
            got(d2t.at[d, at], d2t_r.at[r, d])
        d2s[k, up, at, :] = d2s[k, up, at, :] + d2t[0, at, :]
        put(d2s.at[k, up, at], d2r.at[0, 0, at], d2_r.at[r, 0, 0], (z, col(up, x, k)))
        d2x[down, at, :] = d2x[down, at, :] + d2t[1, at, :]
        put(d2x.at[down, at], d2r.at[1, 1, at], d2_r.at[r, 1, 1], (z, col(down, x, k)))

    low, high = pl.ds(0, 256), pl.ds(256, 256)
    w1_key = len(sent)
    for rows in (low, high, high, low):
        sent.append((lambda: d1t.at[0], None))

    def part_w1(step):
        b = block_at(step)
        for r in range(2):
            d1s[b, pl.ds(r * 256, 256), :] = t_dot(xg[r].reshape(384, 256), dpg[b]).astype(BF)
        total = jnp.sum(dpg[b].astype(F32), axis=0, keepdims=True)
        bs[b] = jnp.broadcast_to(total, (8, 384))
        off = (b - y + 4) % 4

        def go_on(key, rows, dst, sem, dy):
            pltpu.make_async_remote_copy(
                src_ref=d1s.at[b, rows], dst_ref=dst, send_sem=send.at[w1_key + key], recv_sem=sem,
                device_id=(z, col(dy, x, k)), device_id_type=MESH,
            ).start()

        @pl.when(off == 2)
        def _():
            go_on(0, low, d1t.at[0], d1t_r.at[0], up)
            go_on(1, high, d1t.at[1], d1t_r.at[1], down)

        @pl.when(off == 1)
        def _():
            go_on(2, high, d1r.at[0, high], d1_r.at[0, 0], up)

        @pl.when(off == 3)
        def _():
            go_on(3, low, d1r.at[1, low], d1_r.at[1, 0], down)

    def pass_on(cond, back_by, all_rows):
        for n in range(4):
            for s, q in ways:
                j = halves(q)[n]
                block = dpg.at[block_at(-s * back_by), piece(j)]
                sem = dp_r.at[block_at(-s * back_by), j]
                got(block, sem)
                if all_rows or n < 2:
                    put(block, block, sem, ahead[q], cond, lambda: dpg.at[0, piece(0)])

    @pl.when(other)
    def _():
        pass_on(other, 1, True)
        part_w1(1)
        part_w1(-1)

    @pl.when(owner)
    def _():
        part_w1(0)
        pass_on(owner, 2, True)
        part_w1(2)
        part_w1(-2)

    got(hg.at[0], h_r.at[0])
    part_w2(1 - k, 0)
    swap_w2(0)
    part_w2(k, 0)
    pl.when(other)(lambda: pass_on(other, 3, False))
    hop_one_w2(0)

    got(hg.at[1], h_r.at[1])

    def part_out(i, slot):
        o = dot(hg[0], w2g[i, :384, :]) + dot(hg[1], w2g[i, 384:, :])
        for j in range(4):
            ys[slot, j] = o[:, j * 128:(j + 1) * 128].astype(BF)

    part_w2(1 - k, 1)
    swap_w2(1)
    part_w2(k, 1)
    part_out(1 - k, 0)
    put(ys.at[0], yx, yx_r, (z, col(y, x, 1 - k)))
    hop_one_w2(1)
    part_out(k, 1)
    hop_two_w2(0)
    got(yx, yx_r)
    for j in range(4):
        ys[1, j] = ys[1, j] + yx[j]
    keep(ys.at[1, y], ya.at[y], y1_r.at[y])
    for i in (1, 3, 2):
        put(ys.at[1, (y + i) % 4], ya.at[y], y1_r.at[y], (z, col((y + i) % 4, x, k)))

    @pl.when(owner)
    def _():
        for j in range(4):
            got(dpg.at[block_at(4), piece(j)], dp_r.at[block_at(4), j])

    for i in range(2):
        o = dot_t(dpg[0], w1g[0, pl.ds(i * 256, 256), :])
        for j in range(1, 4):
            o = o + dot_t(dpg[j], w1g[j, pl.ds(i * 256, 256), :])
        dxs[i] = o.astype(BF).reshape(2, 4, 48, 256)
    for i in range(4):
        for d in range(2):
            dx, dk = (x + i) % 4, (k + d) % 2
            if i or d:
                put(dxs.at[dk, :, dx], dxr.at[x, k], dx1_r.at[x, k], (z, col(y, dx, dk)))
            else:
                keep(dxs.at[dk, :, dx], dxr.at[x, k], dx1_r.at[x, k])

    @pl.when(owner)
    def _():
        part_w1(4)

    @pl.when(other)
    def _():
        part_w1(3)
        part_w1(-3)

    keep(bs.at[y], dbr.at[y], db_r.at[y])
    for i in (1, 3, 2):
        dy = (y + i) % 4
        put(bs.at[dy], dbr.at[y], db_r.at[y], (z, col(dy, x, k)))

    hop_two_w2(1)

    for i in range(4):
        got(ya.at[i], y1_r.at[i])
    for i in range(8):
        j = (z + i) % 8
        rows = pl.ds(pl.multiple_of(j % 2 * 192, 192), 192)
        if i:
            put(ya.at[j // 2, rows], yr.at[z], y2_r.at[z], (j, c))
        else:
            keep(ya.at[j // 2, rows], yr.at[z], y2_r.at[z])

    for i in range(4):
        for d in range(2):
            got(dxr.at[i, d], dx1_r.at[i, d])
    for h in range(2):
        o = dxr[0, 0, h].astype(F32)
        for j in range(1, 8):
            o = o + dxr[j // 2, j % 2, h].astype(F32)
        for d in range(2):
            dxb[h, d] = o[:, d * 128:(d + 1) * 128].astype(BF)
    for h in range(2):
        for d in range(2):
            dev = back[2 * h + d]
            put_any(
                dxb.at[h, d], ot.at[lanes(x, 48)], dx2_r.at[x], dev,
                jnp.logical_and(dev[0] == z, dev[1] == c),
            )

    for d, (dy, rows) in enumerate(((up, low), (down, high))):
        got(d1t.at[d], d1t_r.at[d])
        d1s[dy, rows, :] = d1s[dy, rows, :] + d1t[d]
        put(d1s.at[dy, rows], d1r.at[d, rows], d1_r.at[d, 1], (z, col(dy, x, k)))

    for r in range(2):
        for i in range(2):
            for d in range(2):
                got(d2r.at[i, d, half_rows(r)], d2_r.at[r, i, d])

    def sum_w2(i, _):
        rows = pl.ds(pl.multiple_of(i * 64, 64), 64)
        for d, local in enumerate((d2s.at[k, y], d2x.at[y])):
            o = local[rows, :].astype(F32)
            for j in range(2):
                o = o + d2r[j, d, rows, :].astype(F32)
            start = (k if d == 0 else 1 - k) * 768 + i * 64
            r_w2[pl.ds(pl.multiple_of(start, 64), 64), :] = o
        return 0

    lax.fori_loop(0, 12, sum_w2, 0)
    keep(r_w2, out_w2, out_r.at[0])
    for i in range(8):
        got(yr.at[i], y2_r.at[i])
    o = yr[0].astype(F32)
    for j in range(1, 8):
        o = o + yr[j].astype(F32)
    r_y[...] = o.astype(BF)
    keep(r_y, out_y, out_r.at[1])
    for i in range(4):
        got(ot.at[pl.ds(i * 48, 48)], dx2_r.at[i])
    keep(ot, out_x, out_r.at[2])
    for i in range(4):
        got(dbr.at[i], db_r.at[i])
    for d, rows in enumerate((high, low)):
        got(d1r.at[d, rows], d1_r.at[d, 0])
        rest = low if d == 0 else high
        got(d1r.at[d, rest], d1_r.at[d, 1])

    def sum_w1(i, _):
        rows = pl.ds(pl.multiple_of(i * 32, 32), 32)
        o = d1s[y, rows, :].astype(F32)
        for j in range(2):
            o = o + d1r[j, rows, :].astype(F32)
        r_w1[rows, :] = o
        return 0

    lax.fori_loop(0, 16, sum_w1, 0)
    keep(r_w1, out_w1, out_r.at[3])
    r_b[...] = dbr[0] + dbr[1] + dbr[2] + dbr[3]
    keep(r_b, out_b, out_r.at[4])
    for i, ref in enumerate((out_w2, out_y, out_x, out_w1, out_b)):
        got(ref, out_r.at[i])

    for i, (like, cond) in enumerate(sent):
        ref = like()
        wait = pltpu.make_async_copy(ref, ref, send.at[i]).wait
        if cond is None:
            wait()
        else:
            pl.when(cond)(wait)


def hand_over(*refs):
    stage, sems = refs[10:14], refs[14]
    parts = []
    for n, i in enumerate((2, 4, 0, 1)):
        rows = refs[i].shape[0] // 2
        for half in range(2):
            at = pl.ds(half * rows, rows)
            key = 2 * n + half
            parts.append((
                pltpu.make_async_copy(refs[i].at[at], stage[n].at[at], sems.at[0, key]),
                pltpu.make_async_copy(stage[n].at[at], refs[5 + i].at[at], sems.at[1, key]),
            ))
    for into, _ in parts:
        into.start()
    refs[8][...] = refs[3][0]
    for into, away in parts:
        into.wait()
        away.start()
    for _, away in parts:
        away.wait()


SENDS = 260
DMA = pltpu.SemaphoreType.DMA


def per_device(tokens, w_in, bias_in, w_out, grad_out):
    vm = pltpu.VMEM
    spec = pl.BlockSpec(memory_space=pltpu.VMEM)
    away = pl.BlockSpec(memory_space=pl.ANY)
    shapes = [
        ((192, 128), BF), ((192, 128), BF), ((512, 384), F32), ((8, 384), F32), ((1536, 128), F32),
    ]
    out = pl.pallas_call(
        kernel,
        out_shape=[jax.ShapeDtypeStruct(s, d) for s, d in shapes],
        in_specs=[away, away, spec, away, away],
        out_specs=[away] * 5,
        scratch_shapes=[
            vm((2, 48, 256), BF),
            vm((2, 2, 4, 48, 256), BF),
            vm((4, 512, 384), BF),
            vm((768, 128), BF),
            vm((2, 768, 512), BF),
            vm((8, 192, 128), BF),
            vm((2, 2, 192, 512), BF),
            vm((8, 384), F32),
            vm((4, 8, 384), F32),
            vm((4, 384, 384), BF),
            vm((2, 2, 384, 384), BF),
            vm((2, 2, 384, 384), BF),
            vm((2, 384, 384), BF),
            vm((4, 384, 384), BF),
            vm((384, 384), BF),
            vm((2, 384, 384), BF),
            vm((4, 384, 384), BF),
            vm((2, 4, 384, 128), BF),
            vm((4, 384, 128), BF),
            vm((4, 384, 128), BF),
            vm((8, 192, 128), BF),
            vm((2, 4, 768, 128), BF),
            vm((4, 768, 128), BF),
            vm((2, 768, 128), BF),
            vm((2, 2, 768, 128), BF),
            vm((2, 2, 4, 48, 256), BF),
            vm((4, 2, 2, 48, 256), BF),
            vm((2, 2, 48, 128), BF),
            vm((192, 128), BF),
            vm((4, 512, 384), BF),
            vm((2, 256, 384), BF),
            vm((2, 512, 384), BF),
            vm((4, 8, 384), F32),
            vm((4, 8, 384), F32),
            vm((192, 128), BF),
            vm((512, 384), F32),
            vm((1536, 128), F32),
            vm((8, 384), F32),
            DMA((SENDS,)),
            DMA((2, 2)), DMA((4, 2)), DMA((4, 2)), DMA, DMA, DMA((4, 2, 2)), DMA((4,)),
            DMA((8,)), DMA((4,)), DMA, DMA((2, 2, 4)), DMA((4,)), DMA((2,)), DMA((4, 4)),
            DMA, DMA((4,)), DMA((8,)), DMA((2, 4)), DMA((2, 2)), DMA((2, 2, 2)), DMA((4, 2)), DMA((4,)),
            DMA((2,)), DMA((2, 2)), DMA((4,)), DMA((5,)),
        ],
        compiler_params=pltpu.CompilerParams(
            collective_id=0, has_side_effects=True, vmem_limit_bytes=56 * 2**20
        ),
        name="mlp_grad",
    )(tokens, w_in, bias_in, w_out, grad_out)
    final = [s if i != 3 else ((384,), F32) for i, s in enumerate(shapes)]
    places = [spec if i == 3 else away for i in range(5)]
    return tuple(
        pl.pallas_call(
            hand_over,
            out_shape=[jax.ShapeDtypeStruct(s, d) for s, d in final],
            in_specs=places,
            out_specs=places,
            scratch_shapes=[vm(*shapes[i]) for i in (2, 4, 0, 1)] + [DMA((2, 8))],
            name="hand_over",
        )(*out)
    )


def solution(mesh):
    return jax.shard_map(
        per_device,
        mesh=mesh,
        in_specs=(P("row", "col"), P("row", "col"), P("col"), P("row", "col"), P("row", "col")),
        out_specs=(P("row", "col"), P("row", "col"), P("row", "col"), P("col"), P("row", "col")),
        check_vma=False,
    )
```

```python
import functools

import jax
import jax.numpy as jnp
from jax import lax
from jax.experimental import pallas as pl
from jax.experimental.pallas import tpu as pltpu
from jax.sharding import PartitionSpec as P

MESH = pl.DeviceIdType.MESH
BF, F32 = jnp.bfloat16, jnp.float32
S2PI = 0.7978845608028654
CUBIC = 0.044715


def dot(a, b):
    return lax.dot_general(a, b, (((1,), (0,)), ((), ())), preferred_element_type=F32)


def dot_t(a, b):
    return lax.dot_general(a, b, (((1,), (1,)), ((), ())), preferred_element_type=F32)


def t_dot(a, b):
    return lax.dot_general(a, b, (((0,), (0,)), ((), ())), preferred_element_type=F32)


def col(y, x, k):
    return y * 8 + x * 2 + k


def lanes(i, n):
    return pl.ds(pl.multiple_of(i * n, n), n)


def kernel(
    tok, w1, bias, w2, go,
    out_y, out_x, out_w1, out_b, out_w2,
    xa, xg, w1g, w2h, w2g, gs, gg, b8, bg,
    ps, rz, tz, dhs, dhr, ho, hg, dpg,
    ys, yx, ya, yr, d2s, d2x, d2t, d2r, dxs, dxr, dxb, ot, d1s, d1t, d1r, bs, dbr, r_y, r_w1, r_w2, r_b,
    send, x1_r, x2_r, w1_r, w2s_r, w2k_r, w2_r, b_r, g1_r, g2_r, g3_r, p_r, dh_r, h_r, dp_r,
    yx_r, y1_r, y2_r, d2x_r, d2t_r, d2_r, dx1_r, dx2_r, d1t_r, d1_r, db_r, out_r,
):
    z, c = lax.axis_index("row"), lax.axis_index("col")
    k, x, y = c % 2, (c // 2) % 4, c // 8
    sent = []

    def put(src, dst, rsem, dev, cond=None, like=None):
        copy = pltpu.make_async_remote_copy(
            src_ref=src, dst_ref=dst, send_sem=send.at[len(sent)], recv_sem=rsem,
            device_id=dev, device_id_type=MESH,
        )
        if cond is None or like is not None:
            copy.start()
        else:
            pl.when(cond)(copy.start)
        sent.append((like or (lambda: src), cond))

    def put_any(src, dst, rsem, dev, here):
        put(src, dst, rsem, dev, jnp.logical_not(here))
        pl.when(here)(pltpu.make_async_copy(src, dst, rsem).start)

    def keep(src, dst, rsem):
        pltpu.make_async_copy(src, dst, rsem).start()

    def got(dst, rsem):
        pltpu.make_async_copy(dst, dst, rsem).wait()

    barrier = pltpu.get_barrier_semaphore()
    near = [((z + i) % 8, c) for i in range(1, 8)]
    near += [(z, col((y + i) % 4, x, (k + d) % 2)) for i in range(4) for d in range(2) if i or d]
    near += [(z, col(y, (x + i) % 4, (k + d) % 2)) for i in range(1, 4) for d in range(2)]
    far = [(2 * y + x // 2, col(z // 2, j, x % 2)) for j in range(4)]
    back = [(2 * y + h, col(z // 2, 2 * (z % 2) + k, d)) for h in range(2) for d in range(2)]
    for dev in near + far + back:
        pl.semaphore_signal(barrier, inc=1, device_id=dev, device_id_type=MESH)
    pl.semaphore_wait(barrier, len(near + far + back))

    for j in range(4):
        here = jnp.logical_and(far[j][0] == z, far[j][1] == c)
        put_any(
            tok.at[pl.ds(j * 48, 48)], xa.at[z % 2, :, lanes(k, 128)], x1_r.at[z % 2, k], far[j], here
        )
    keep(go, gs.at[z], g1_r.at[z])
    for i in (4, 3, 5, 2, 6, 1, 7):
        put(go, gs.at[z], g1_r.at[z], ((z + i) % 8, c))
    up, down = (y + 1) % 4, (y + 3) % 4
    b8[...] = jnp.broadcast_to(bias[...].reshape(1, 384), b8.shape)
    for i in range(2):
        rows = pl.ds(i * 256, 256)
        keep(w1.at[rows], w1g.at[y, rows], w1_r.at[y, i])
    for i in range(2):
        for n, dy in enumerate((up, down)):
            rows = pl.ds((i ^ n) * 256, 256)
            put(w1.at[rows], w1g.at[y, rows], w1_r.at[y, i ^ n], (z, col(dy, x, k)))
    mine = pl.ds(pl.multiple_of(k * 768, 768), 768)
    theirs = pl.ds(pl.multiple_of((1 - k) * 768, 768), 768)
    put(w2.at[theirs], w2h, w2s_r, (z, col(y, x, 1 - k)))
    keep(w2.at[mine], w2g.at[k, :, lanes(y, 128)], w2k_r)
    keep(b8, bg.at[y], b_r.at[y])
    for i in (1, 2, 3):
        put(b8, bg.at[y], b_r.at[y], (z, col((y + i) % 4, x, k)))
    for h in range(2):
        for d in range(2):
            got(xa.at[h, :, pl.ds(d * 128, 128)], x1_r.at[h, d])
    keep(xa, xg.at[k, :, x], x2_r.at[x, k])
    for i in range(4):
        for d in range(2):
            if i or d:
                put(xa, xg.at[k, :, x], x2_r.at[x, k], (z, col(y, (x + i) % 4, (k + d) % 2)))

    for i, (dy, fy) in enumerate(((up, down), (down, up))):
        rows = pl.ds(i * 256, 256)
        got(w1g.at[fy, rows], w1_r.at[fy, i])
        put(w1g.at[fy, rows], w1g.at[fy, rows], w1_r.at[fy, i], (z, col(dy, x, k)))
    got(w2h, w2s_r)
    keep(w2h, w2g.at[1 - k, :, lanes(y, 128)], w2s_r)

    def start_w2(i):
        for dy in (up, down):
            rows = pl.ds(pl.multiple_of(k * 768 + i * 384, 384), 384)
            put(
                w2.at[rows], w2g.at[k, pl.ds(i * 384, 384), lanes(y, 128)], w2_r.at[y, k, i],
                (z, col(dy, x, k)),
            )
            rows = pl.ds(i * 384, 384)
            put(
                w2h.at[rows], w2g.at[1 - k, rows, lanes(y, 128)], w2_r.at[y, 1 - k, i],
                (z, col(dy, x, k)),
            )

    start_w2(0)

    def pass_w2(i):
        for d, (dy, fy) in enumerate(((up, down), (down, up))):
            block = w2g.at[d, pl.ds(i * 384, 384), lanes(fy, 128)]
            got(block, w2_r.at[fy, d, i])
            put(block, block, w2_r.at[fy, d, i], (z, col(dy, x, k)))

    for i in range(8):
        got(gs.at[i], g1_r.at[i])
    for i in (2, 1, 3, 0):
        dy = (y + i) % 4
        src, dst = gs.at[pl.ds(2 * dy, 2)], gg.at[k, :, :, lanes(y, 128)]
        if i:
            put(src, dst, g2_r.at[y], (z, col(dy, x, k)))
        else:
            keep(src, dst, g2_r.at[y])

    for i in range(4):
        for d in range(2):
            got(xg.at[d, :, i], x2_r.at[i, d])
    got(w1g.at[y, pl.ds(0, 256)], w1_r.at[y, 0])
    got(w1g.at[y, pl.ds(256, 256)], w1_r.at[y, 1])
    got(w1g.at[down, pl.ds(256, 256)], w1_r.at[down, 1])
    got(w1g.at[up, pl.ds(0, 256)], w1_r.at[up, 0])
    for i in range(2):
        got(w1g.at[(y + 2) % 4, pl.ds(i * 256, 256)], w1_r.at[(y + 2) % 4, i])

    owner = z % 2 == x // 2
    other = jnp.logical_not(owner)
    odd = (z + x // 2) % 2
    ways = ((1, 0), (-1, 1))
    ahead = [((z + 1) % 8, c), ((z + 7) % 8, c)]

    def block_at(step):
        return ((z + step + 16) % 8) // 2

    first = [block_at(s * (4 - odd)) for s, _ in ways]
    second = [block_at(s * (2 - odd)) for s, _ in ways]

    def piece(j):
        return pl.ds(j * 96, 96)

    def halves(q):
        return (2, 3, 0, 1) if q else (0, 1, 2, 3)

    def part(i, _):
        x0 = xg[0].reshape(384, 256)
        x1 = xg[1].reshape(384, 256)
        ps[i] = (dot(x0, w1g[i, :256]) + dot(x1, w1g[i, 256:])).astype(BF)
        return 0

    lax.fori_loop(0, 4, part, 0)
    for n in range(2):
        for _, q in ways:
            for cond, j in ((owner, halves(q)[n]), (other, halves(q)[2 + n])):
                put(
                    ps.at[first[q], piece(j)], rz.at[q, 0, piece(j)], p_r.at[q, 0, j],
                    ahead[q], cond,
                )
    home = 2 * (z % 2) + k

    def part_hidden(i):
        for d in range(2):
            for j in (down if d else up, (y + 2) % 4):
                got(w2g.at[d, pl.ds(i * 384, 384), lanes(j, 128)], w2_r.at[j, d, i])
        rows = pl.ds(i * 384, 384)
        g0 = gg[0].reshape(384, 512)
        g1 = gg[1].reshape(384, 512)
        dhs[i] = (dot_t(g0, w2g[0, rows, :]) + dot_t(g1, w2g[1, rows, :])).astype(BF)
        put_any(
            dhs.at[i], dhr.at[x], dh_r.at[x], (z, col(y, home, i)),
            jnp.logical_and(home == x, k == i),
        )

    def relay(cond, mine, kind, to, n, q):
        j = (halves(q) if kind == to == 0 else halves(1 - q))[n]
        got(rz.at[q, kind, piece(j)], p_r.at[q, kind, j])
        tz[q, to, piece(j), :] = ps[mine, piece(j), :] + rz[q, kind, piece(j), :]
        put(
            tz.at[q, to, piece(j)], rz.at[q, to, piece(j)], p_r.at[q, to, j], ahead[q], cond,
            lambda: tz.at[q, to, piece(j)],
        )

    for i in range(4):
        got(gg.at[k, :, :, pl.ds(i * 128, 128)], g2_r.at[i])
    put(gg.at[k], gg.at[k], g3_r, (z, col(y, x, 1 - k)))

    pass_w2(0)
    start_w2(1)

    @pl.when(other)
    def _():
        for n in range(2):
            for _, q in ways:
                relay(other, first[q], 0, 0, n, q)

    @pl.when(owner)
    def _():
        for n in range(2):
            for _, q in ways:
                relay(owner, second[q], 0, 1, n, q)

    got(gg.at[1 - k], g3_r)
    got(w2g.at[k, :, lanes(y, 128)], w2k_r)
    got(w2g.at[1 - k, :, lanes(y, 128)], w2s_r)
    part_hidden(0)

    @pl.when(owner)
    def _():
        for n in range(2, 4):
            for _, q in ways:
                relay(owner, second[q], 0, 1, n, q)

    pass_w2(1)

    @pl.when(other)
    def _():
        for n in range(4):
            for _, q in ways:
                relay(other, second[q], 1, 1, n, q)

    part_hidden(1)

    @pl.when(owner)
    def _():
        for i in range(4):
            got(bg.at[i], b_r.at[i])
        for j in range(4):
            for _, q in ways:
                got(rz.at[q, 1, piece(j)], p_r.at[q, 1, j])
        for i in range(4):
            got(dhr.at[i], dh_r.at[i])

        def point(i, _):
            rows = pl.ds(pl.multiple_of(i * 16, 16), 16)
            v = jnp.broadcast_to(bg[z // 2, pl.ds(0, 1), :], (16, 384))
            v = v + ps[z // 2, rows, :].astype(F32)
            v = v + (rz[0, 1, rows, :].astype(F32) + rz[1, 1, rows, :].astype(F32))
            grad = dhr[0, rows, :].astype(F32)
            for j in range(1, 4):
                grad = grad + dhr[j, rows, :].astype(F32)
            v2 = v * v
            t = jnp.tanh(S2PI * (v + CUBIC * (v2 * v)))
            cdf = 0.5 * (1.0 + t)
            ho[rows, :] = (v * cdf).astype(BF)
            slope = cdf + (0.5 * v) * (1.0 - t * t) * (S2PI * (1.0 + 3.0 * CUBIC * v2))
            dpg[z // 2, rows, :] = (grad * slope).astype(BF)
            return 0

        lax.fori_loop(0, 24, point, 0)

    @pl.when(jnp.logical_not(owner))
    def _():
        for i in range(4):
            got(bg.at[i], b_r.at[i])

    for i in (2, 1, 3, 0):
        here = jnp.logical_and((x + i) % 4 == x, x % 2 == k)
        put(
            ho, hg.at[k], h_r.at[k], (z, col(y, (x + i) % 4, x % 2)),
            jnp.logical_and(owner, jnp.logical_not(here)),
        )
        pl.when(jnp.logical_and(owner, here))(
            pltpu.make_async_copy(ho, hg.at[k], h_r.at[k]).start
        )

    @pl.when(owner)
    def _():
        for n in range(4):
            for _, q in ways:
                block = dpg.at[z // 2, piece(halves(q)[n])]
                put(block, block, dp_r.at[z // 2, halves(q)[n]], ahead[q], owner, lambda: dpg.at[0, piece(0)])

    far_y = (y + 2) % 4

    def half_rows(r):
        return pl.ds(r * 384, 384)

    def part_w2(i, r):
        o = t_dot(hg[r], gg[i].reshape(384, 512))
        for j in range(4):
            d2s[i, j, half_rows(r), :] = o[:, j * 128:(j + 1) * 128].astype(BF)

    def swap_w2(r):
        for i in (2, 1, 3, 0):
            j = (y + i) % 4
            put(
                d2s.at[1 - k, j, half_rows(r)], d2x.at[j, half_rows(r)], d2x_r.at[r, j],
                (z, col(y, x, 1 - k)),
            )

    def hop_one_w2(r):
        at = half_rows(r)
        for i in (2, 1, 3, 0):
            got(d2x.at[(y + i) % 4, at], d2x_r.at[r, (y + i) % 4])
        put(d2s.at[k, far_y, at], d2t.at[0, at], d2t_r.at[r, 0], (z, col(up, x, k)))
        put(d2x.at[far_y, at], d2t.at[1, at], d2t_r.at[r, 1], (z, col(down, x, k)))
        put(d2x.at[up, at], d2r.at[0, 1, at], d2_r.at[r, 0, 1], (z, col(up, x, k)))
        put(d2s.at[k, down, at], d2r.at[1, 0, at], d2_r.at[r, 1, 0], (z, col(down, x, k)))

    def hop_two_w2(r):
        at = half_rows(r)
        for d in range(2):
            got(d2t.at[d, at], d2t_r.at[r, d])
        d2s[k, up, at, :] = d2s[k, up, at, :] + d2t[0, at, :]
        put(d2s.at[k, up, at], d2r.at[0, 0, at], d2_r.at[r, 0, 0], (z, col(up, x, k)))
        d2x[down, at, :] = d2x[down, at, :] + d2t[1, at, :]
        put(d2x.at[down, at], d2r.at[1, 1, at], d2_r.at[r, 1, 1], (z, col(down, x, k)))

    low, high = pl.ds(0, 256), pl.ds(256, 256)
    w1_key = len(sent)
    for rows in (low, high, high, low):
        sent.append((lambda: d1t.at[0], None))

    def part_w1(step):
        b = block_at(step)
        for r in range(2):
            d1s[b, pl.ds(r * 256, 256), :] = t_dot(xg[r].reshape(384, 256), dpg[b]).astype(BF)
        total = jnp.sum(dpg[b].astype(F32), axis=0, keepdims=True)
        bs[b] = jnp.broadcast_to(total, (8, 384))
        off = (b - y + 4) % 4

        def go_on(key, rows, dst, sem, dy):
            pltpu.make_async_remote_copy(
                src_ref=d1s.at[b, rows], dst_ref=dst, send_sem=send.at[w1_key + key], recv_sem=sem,
                device_id=(z, col(dy, x, k)), device_id_type=MESH,
            ).start()

        @pl.when(off == 2)
        def _():
            go_on(0, low, d1t.at[0], d1t_r.at[0], up)
            go_on(1, high, d1t.at[1], d1t_r.at[1], down)

        @pl.when(off == 1)
        def _():
            go_on(2, high, d1r.at[0, high], d1_r.at[0, 0], up)

        @pl.when(off == 3)
        def _():
            go_on(3, low, d1r.at[1, low], d1_r.at[1, 0], down)

    def pass_on(cond, back_by, all_rows):
        for n in range(4):
            for s, q in ways:
                j = halves(q)[n]
                block = dpg.at[block_at(-s * back_by), piece(j)]
                sem = dp_r.at[block_at(-s * back_by), j]
                got(block, sem)
                if all_rows or n < 2:
                    put(block, block, sem, ahead[q], cond, lambda: dpg.at[0, piece(0)])

    @pl.when(other)
    def _():
        pass_on(other, 1, True)
        part_w1(1)
        part_w1(-1)

    @pl.when(owner)
    def _():
        part_w1(0)
        pass_on(owner, 2, True)
        part_w1(2)
        part_w1(-2)

    got(hg.at[0], h_r.at[0])
    part_w2(1 - k, 0)
    swap_w2(0)
    part_w2(k, 0)
    pl.when(other)(lambda: pass_on(other, 3, False))
    hop_one_w2(0)

    got(hg.at[1], h_r.at[1])

    def part_out(i, slot):
        o = dot(hg[0], w2g[i, :384, :]) + dot(hg[1], w2g[i, 384:, :])
        for j in range(4):
            ys[slot, j] = o[:, j * 128:(j + 1) * 128].astype(BF)

    part_w2(1 - k, 1)
    swap_w2(1)
    part_w2(k, 1)
    part_out(1 - k, 0)
    put(ys.at[0], yx, yx_r, (z, col(y, x, 1 - k)))
    hop_one_w2(1)
    part_out(k, 1)
    hop_two_w2(0)
    got(yx, yx_r)
    for j in range(4):
        ys[1, j] = ys[1, j] + yx[j]
    keep(ys.at[1, y], ya.at[y], y1_r.at[y])
    for i in (1, 3, 2):
        put(ys.at[1, (y + i) % 4], ya.at[y], y1_r.at[y], (z, col((y + i) % 4, x, k)))

    @pl.when(owner)
    def _():
        for j in range(4):
            got(dpg.at[block_at(4), piece(j)], dp_r.at[block_at(4), j])

    for i in range(2):
        o = dot_t(dpg[0], w1g[0, pl.ds(i * 256, 256), :])
        for j in range(1, 4):
            o = o + dot_t(dpg[j], w1g[j, pl.ds(i * 256, 256), :])
        dxs[i] = o.astype(BF).reshape(2, 4, 48, 256)
    for i in range(4):
        for d in range(2):
            dx, dk = (x + i) % 4, (k + d) % 2
            if i or d:
                put(dxs.at[dk, :, dx], dxr.at[x, k], dx1_r.at[x, k], (z, col(y, dx, dk)))
            else:
                keep(dxs.at[dk, :, dx], dxr.at[x, k], dx1_r.at[x, k])

    @pl.when(owner)
    def _():
        part_w1(4)

    @pl.when(other)
    def _():
        part_w1(3)
        part_w1(-3)

    keep(bs.at[y], dbr.at[y], db_r.at[y])
    for i in (1, 3, 2):
        dy = (y + i) % 4
        put(bs.at[dy], dbr.at[y], db_r.at[y], (z, col(dy, x, k)))

    hop_two_w2(1)

    for i in range(4):
        got(ya.at[i], y1_r.at[i])
    for i in range(8):
        j = (z + i) % 8
        rows = pl.ds(pl.multiple_of(j % 2 * 192, 192), 192)
        if i:
            put(ya.at[j // 2, rows], yr.at[z], y2_r.at[z], (j, c))
        else:
            keep(ya.at[j // 2, rows], yr.at[z], y2_r.at[z])

    for i in range(4):
        for d in range(2):
            got(dxr.at[i, d], dx1_r.at[i, d])
    for h in range(2):
        o = dxr[0, 0, h].astype(F32)
        for j in range(1, 8):
            o = o + dxr[j // 2, j % 2, h].astype(F32)
        for d in range(2):
            dxb[h, d] = o[:, d * 128:(d + 1) * 128].astype(BF)
    for h in range(2):
        for d in range(2):
            dev = back[2 * h + d]
            put_any(
                dxb.at[h, d], ot.at[lanes(x, 48)], dx2_r.at[x], dev,
                jnp.logical_and(dev[0] == z, dev[1] == c),
            )

    for d, (dy, rows) in enumerate(((up, low), (down, high))):
        got(d1t.at[d], d1t_r.at[d])
        d1s[dy, rows, :] = d1s[dy, rows, :] + d1t[d]
        put(d1s.at[dy, rows], d1r.at[d, rows], d1_r.at[d, 1], (z, col(dy, x, k)))

    for r in range(2):
        for i in range(2):
            for d in range(2):
                got(d2r.at[i, d, half_rows(r)], d2_r.at[r, i, d])

    def sum_w2(i, _):
        rows = pl.ds(pl.multiple_of(i * 64, 64), 64)
        for d, local in enumerate((d2s.at[k, y], d2x.at[y])):
            o = local[rows, :].astype(F32)
            for j in range(2):
                o = o + d2r[j, d, rows, :].astype(F32)
            start = (k if d == 0 else 1 - k) * 768 + i * 64
            r_w2[pl.ds(pl.multiple_of(start, 64), 64), :] = o
        return 0

    lax.fori_loop(0, 12, sum_w2, 0)
    keep(r_w2, out_w2, out_r.at[0])
    for i in range(8):
        got(yr.at[i], y2_r.at[i])
    o = yr[0].astype(F32)
    for j in range(1, 8):
        o = o + yr[j].astype(F32)
    r_y[...] = o.astype(BF)
    keep(r_y, out_y, out_r.at[1])
    for i in range(4):
        got(ot.at[pl.ds(i * 48, 48)], dx2_r.at[i])
    keep(ot, out_x, out_r.at[2])
    for i in range(4):
        got(dbr.at[i], db_r.at[i])
    for d, rows in enumerate((high, low)):
        got(d1r.at[d, rows], d1_r.at[d, 0])
        rest = low if d == 0 else high
        got(d1r.at[d, rest], d1_r.at[d, 1])

    def sum_w1(i, _):
        rows = pl.ds(pl.multiple_of(i * 32, 32), 32)
        o = d1s[y, rows, :].astype(F32)
        for j in range(2):
            o = o + d1r[j, rows, :].astype(F32)
        r_w1[rows, :] = o
        return 0

    lax.fori_loop(0, 16, sum_w1, 0)
    keep(r_w1, out_w1, out_r.at[3])
    r_b[...] = dbr[0] + dbr[1] + dbr[2] + dbr[3]
    keep(r_b, out_b, out_r.at[4])
    for i, ref in enumerate((out_w2, out_y, out_x, out_w1, out_b)):
        got(ref, out_r.at[i])

    for i, (like, cond) in enumerate(sent):
        ref = like()
        wait = pltpu.make_async_copy(ref, ref, send.at[i]).wait
        if cond is None:
            wait()
        else:
            pl.when(cond)(wait)


def hand_over(*refs):
    stage, sems = refs[10:14], refs[14]
    parts = []
    for n, i in enumerate((2, 4, 0, 1)):
        rows = refs[i].shape[0] // 2
        for half in range(2):
            at = pl.ds(half * rows, rows)
            key = 2 * n + half
            parts.append((
                pltpu.make_async_copy(refs[i].at[at], stage[n].at[at], sems.at[0, key]),
                pltpu.make_async_copy(stage[n].at[at], refs[5 + i].at[at], sems.at[1, key]),
            ))
    for into, _ in parts:
        into.start()
    refs[8][...] = refs[3][0]
    for into, away in parts:
        into.wait()
        away.start()
    for _, away in parts:
        away.wait()


SENDS = 260
DMA = pltpu.SemaphoreType.DMA


def per_device(tokens, w_in, bias_in, w_out, grad_out):
    vm = pltpu.VMEM
    spec = pl.BlockSpec(memory_space=pltpu.VMEM)
    away = pl.BlockSpec(memory_space=pl.ANY)
    shapes = [
        ((192, 128), BF), ((192, 128), BF), ((512, 384), F32), ((8, 384), F32), ((1536, 128), F32),
    ]
    out = pl.pallas_call(
        kernel,
        out_shape=[jax.ShapeDtypeStruct(s, d) for s, d in shapes],
        in_specs=[away, away, spec, away, away],
        out_specs=[away] * 5,
        scratch_shapes=[
            vm((2, 48, 256), BF),
            vm((2, 2, 4, 48, 256), BF),
            vm((4, 512, 384), BF),
            vm((768, 128), BF),
            vm((2, 768, 512), BF),
            vm((8, 192, 128), BF),
            vm((2, 2, 192, 512), BF),
            vm((8, 384), F32),
            vm((4, 8, 384), F32),
            vm((4, 384, 384), BF),
            vm((2, 2, 384, 384), BF),
            vm((2, 2, 384, 384), BF),
            vm((2, 384, 384), BF),
            vm((4, 384, 384), BF),
            vm((384, 384), BF),
            vm((2, 384, 384), BF),
            vm((4, 384, 384), BF),
            vm((2, 4, 384, 128), BF),
            vm((4, 384, 128), BF),
            vm((4, 384, 128), BF),
            vm((8, 192, 128), BF),
            vm((2, 4, 768, 128), BF),
            vm((4, 768, 128), BF),
            vm((2, 768, 128), BF),
            vm((2, 2, 768, 128), BF),
            vm((2, 2, 4, 48, 256), BF),
            vm((4, 2, 2, 48, 256), BF),
            vm((2, 2, 48, 128), BF),
            vm((192, 128), BF),
            vm((4, 512, 384), BF),
            vm((2, 256, 384), BF),
            vm((2, 512, 384), BF),
            vm((4, 8, 384), F32),
            vm((4, 8, 384), F32),
            vm((192, 128), BF),
            vm((512, 384), F32),
            vm((1536, 128), F32),
            vm((8, 384), F32),
            DMA((SENDS,)),
            DMA((2, 2)), DMA((4, 2)), DMA((4, 2)), DMA, DMA, DMA((4, 2, 2)), DMA((4,)),
            DMA((8,)), DMA((4,)), DMA, DMA((2, 2, 4)), DMA((4,)), DMA((2,)), DMA((4, 4)),
            DMA, DMA((4,)), DMA((8,)), DMA((2, 4)), DMA((2, 2)), DMA((2, 2, 2)), DMA((4, 2)), DMA((4,)),
            DMA((2,)), DMA((2, 2)), DMA((4,)), DMA((5,)),
        ],
        compiler_params=pltpu.CompilerParams(
            collective_id=0, has_side_effects=True, vmem_limit_bytes=56 * 2**20
        ),
        name="mlp_grad",
    )(tokens, w_in, bias_in, w_out, grad_out)
    final = [s if i != 3 else ((384,), F32) for i, s in enumerate(shapes)]
    places = [spec if i == 3 else away for i in range(5)]
    return tuple(
        pl.pallas_call(
            hand_over,
            out_shape=[jax.ShapeDtypeStruct(s, d) for s, d in final],
            in_specs=places,
            out_specs=places,
            scratch_shapes=[vm(*shapes[i]) for i in (2, 4, 0, 1)] + [DMA((2, 8))],
            name="hand_over",
        )(*out)
    )


def solution(mesh):
    return jax.shard_map(
        per_device,
        mesh=mesh,
        in_specs=(P("row", "col"), P("row", "col"), P("col"), P("row", "col"), P("row", "col")),
        out_specs=(P("row", "col"), P("row", "col"), P("row", "col"), P("col"), P("row", "col")),
        check_vma=False,
    )
```
